32 devices in a mesh: dp: 4 (over y, x), fsdp: 8 (over z, core).
Axes of the slice: x: 2, y: 2, z: 4, core: 2. Of those that a mesh axis runs over, the one named last changes fastest.
Arguments:
- signal: bfloat16 [2048, 1024], P(('dp', 'fsdp')), may hold values from -6 to 6
- grad_gated: bfloat16 [2048, 512], P(('dp', 'fsdp')), may hold values from -6 to 6
- conv_weight: bfloat16 [1024, 3072], P('fsdp'), may hold values from -0.109375 to 0.109375
- source_seg: int32 [32, 8], P(('dp', 'fsdp')), may hold values from -1 to 63, as said below
Outputs:
- gated_out: bfloat16 [2048, 512], P(('dp', 'fsdp'))
- grad_in: bfloat16 [2048, 1024], P(('dp', 'fsdp'))
- grad_weight: float32 [1024, 3072], P('fsdp')
The draws below stay inside these ranges and needn't reach their ends.
Inputs may be any that keep to these rules, and one draw needn't show every extreme that they name: `source_seg`: -1 where a stream begins. The preceding segment holds the same position on its device as g on its own, no two segments of one device take their left context from the same device, and every segment precedes at most one segment.
All inputs are finite; a program needn't handle non-finite values.
Results may differ from the reference program's by a relative error of at most 0.0049.
Values may be sent and summed in bfloat16 or wider, within the bound.
No kernel may reach another device: no remote copies, remote signals or barrier semaphores. Data moves between devices by JAX's collectives and lax.ppermute only.
A program may use at most 64 MiB of HBM per device.

```python
import math
import jax
import jax.numpy as jnp
from jax import lax

C = 1024
H = 512
DILATION_SIZE = 4
CONTEXT_ROWS = 8
SEG_LEN = 8
SEGS = 8
TOKENS = 2048
N_DP = 4
N_FSDP = 8


def one_permutation(subkey):
    return jax.random.permutation(subkey, N_FSDP)


def draw_source_seg(key, part):
    base = jax.random.fold_in(key, 7)
    perm_keys = jax.random.split(jax.random.fold_in(base, 1), N_DP)
    shift_amounts = jax.vmap(one_permutation)(perm_keys).astype(jnp.int32)
    begins = jax.random.randint(jax.random.fold_in(base, 2), (N_DP, N_FSDP, SEGS), 0, 5) == 0
    device = jnp.arange(N_FSDP, dtype=jnp.int32)[None, :, None]
    position = jnp.arange(SEGS, dtype=jnp.int32)[None, None, :]
    shift_rows_down = shift_amounts[:, None, :]
    source_dev = (device - shift_rows_down) % N_FSDP
    source = jnp.where(begins, -1, source_dev * SEGS + position)
    return source.reshape(N_DP * N_FSDP, SEGS).astype(jnp.int32)


def spiked(array, rng, source, target, shards_of, factor):
    def block_of(dim):
        return (jnp.arange(array.shape[dim]) // (array.shape[dim] // shards_of)).reshape((-1,) + (1,) * (array.ndim - 1 - dim))

    near = jax.random.permutation(rng, shards_of)[block_of(target)]
    other_side = (block_of(target) + shards_of // 2) % shards_of
    return jnp.where((block_of(source) == near) | (block_of(source) == other_side), factor * array, array)


def block_levels(key, extent, cuts, smallest, largest):
    level, own = 1.0, jax.random.fold_in(key, 6)
    for dim, blocks in cuts:
        draws = jnp.exp(jax.random.uniform(jax.random.fold_in(own, dim), (blocks,), jnp.float32, smallest / len(cuts), largest / len(cuts)))
        level = level * jnp.repeat(draws, extent[dim] // blocks).reshape([-1 if axis == dim else 1 for axis in range(len(extent))])
    return level


def scatter_about(rng, shape, spread, limit, cuts=(), held_as=jnp.bfloat16):
    values = jax.random.normal(rng, shape, jnp.float32) * spread
    if len(cuts) > 0:
        values = block_levels(rng, shape, cuts, -0.22, 0.18) * values
    return jnp.clip(values, min=-limit, max=limit).astype(held_as)


def noise_with(stream_key, extent, deviation, reach, cuts, heavy, kind=jnp.bfloat16):
    values = deviation * jax.random.normal(stream_key, extent, jnp.float32)
    if cuts:
        values = values * block_levels(stream_key, extent, cuts, -0.22, 0.18)
    return jnp.clip(spiked(values, jax.random.fold_in(stream_key, 3), *heavy), -reach, reach).astype(kind)


def setup_inputs(seed: int = 0) -> dict:
    arg_keys = jax.random.split(jax.random.key(seed), 5)
    signal = scatter_about(arg_keys[0], (TOKENS, C), 1.0, 6.0, ((0, 32),))
    grad_gated = noise_with(arg_keys[1], (TOKENS, H), 1.0, 6.0, ((0, 32),), (0, 1, 32, 2.75))
    conv_weight = scatter_about(arg_keys[2], (2 * H, 3 * C), (3 * C) ** -0.5, 0.109375, ((0, 8),))
    source_seg = draw_source_seg(jax.random.fold_in(arg_keys[4], 71), 0)
    return {"signal": signal, "grad_gated": grad_gated, "conv_weight": conv_weight, "source_seg": source_seg}


def tap_starts():
    return [CONTEXT_ROWS - (2 - selected_index) * DILATION_SIZE for selected_index in range(3)]

def reference(signal, grad_gated, conv_weight, source_seg):
    group_segs = N_FSDP * SEGS
    signal_groups = signal.reshape(N_DP, group_segs, SEG_LEN, C)
    grad_groups = grad_gated.reshape(N_DP, group_segs * SEG_LEN, H)
    source_groups = source_seg.reshape(N_DP, group_segs)
    starts = tap_starts()

    def one_group(operands):
        segments, upstream, sources = operands
        tail_rows = segments[:, SEG_LEN - CONTEXT_ROWS:, :]
        has_source = sources >= 0
        picked = jnp.take(tail_rows, jnp.maximum(sources, 0).astype(jnp.int32), axis=0)
        carries = jnp.where(has_source[:, None, None], picked, jnp.zeros_like(picked))
        extended = jnp.concatenate([carries, segments], axis=1)
        stacked = jnp.concatenate([extended[:, start:start + SEG_LEN, :] for start in starts], axis=2)
        stacked = stacked.reshape(group_segs * SEG_LEN, 3 * C)
        preact = jnp.dot(stacked, conv_weight.T, preferred_element_type=jnp.float32)
        filter_act = jnp.tanh(preact[:, :H])
        gate_act = jax.nn.sigmoid(preact[:, H:])
        gated_out = (filter_act * gate_act).astype(jnp.bfloat16)
        upstream_wide = upstream.astype(jnp.float32)
        grad_pre = jnp.concatenate([upstream_wide * gate_act * (1.0 - filter_act * filter_act), upstream_wide * filter_act * gate_act * (1.0 - gate_act)], axis=1).astype(jnp.bfloat16)
        partials = jnp.einsum('drj,drc->djc', grad_pre.reshape(N_FSDP, SEGS * SEG_LEN, 2 * H).astype(jnp.float32), stacked.reshape(N_FSDP, SEGS * SEG_LEN, 3 * C).astype(jnp.float32))
        rounded = lax.optimization_barrier(partials.astype(jnp.bfloat16))
        group_sum = lax.optimization_barrier(jnp.sum(rounded.astype(jnp.float32), axis=0))
        back_proj = jnp.dot(grad_pre, conv_weight, preferred_element_type=jnp.float32)
        back_proj = back_proj.reshape(group_segs, SEG_LEN, 3 * C)
        grad_ext = jnp.zeros((group_segs, CONTEXT_ROWS + SEG_LEN, C), jnp.float32)
        for selected_index, start in enumerate(starts):
            grad_ext = grad_ext.at[:, start:start + SEG_LEN, :].add(back_proj[:, :, selected_index * C:(selected_index + 1) * C])
        carry_grad = jnp.where(has_source[:, None, None], grad_ext[:, :CONTEXT_ROWS, :], jnp.zeros_like(grad_ext[:, :CONTEXT_ROWS, :]))
        target = jnp.where(has_source, sources, group_segs).astype(jnp.int32)
        tail_grad = jax.ops.segment_sum(carry_grad, target, num_segments=group_segs + 1)[:group_segs]
        grad_in = grad_ext[:, CONTEXT_ROWS:, :].at[:, SEG_LEN - CONTEXT_ROWS:, :].add(tail_grad)
        return (gated_out, grad_in.reshape(group_segs * SEG_LEN, C).astype(jnp.bfloat16), group_sum)
    gated_out, grad_in, group_sums = lax.map(one_group, (signal_groups, grad_groups, source_groups))
    grad_weight = lax.optimization_barrier(jnp.sum(group_sums, axis=0)) * (1.0 / math.sqrt(TOKENS))
    return (gated_out.reshape(TOKENS, H), grad_in.reshape(TOKENS, C), grad_weight)
```

```python
import functools
import math

import jax
import jax.numpy as jnp
from jax import lax
from jax.experimental import pallas as pl
from jax.experimental.pallas import tpu as pltpu
from jax.sharding import PartitionSpec as P

C = 1024
H = 512
DILATION_SIZE = 4
SEG = 8
BF16 = jnp.bfloat16
F32 = jnp.float32
VMEM = pl.BlockSpec(memory_space=pltpu.VMEM)
SMEM = pl.BlockSpec(memory_space=pltpu.SMEM)


def swap(value, axis, distance):
    count = lax.axis_size(axis)
    return lax.ppermute(value, axis, [(i, i ^ distance) for i in range(count)])


def call(body, out_shapes, in_specs, scratch=(), out_specs=None, flops=0, moved=0):
    return pl.pallas_call(
        body,
        out_shape=out_shapes,
        in_specs=in_specs,
        out_specs=out_specs if out_specs is not None else [VMEM] * len(out_shapes),
        scratch_shapes=list(scratch),
        compiler_params=pltpu.CompilerParams(vmem_limit_bytes=24 * 1024 * 1024),
        cost_estimate=pl.CostEstimate(flops=flops, bytes_accessed=moved, transcendentals=0),
    )


def shaped(shape, dtype):
    return jax.ShapeDtypeStruct(shape, dtype)


def roll_half(first, second):
    row = lax.broadcasted_iota(jnp.int32, first.shape, 0)
    return pltpu.roll(jnp.where(row >= 4, first, second), 4, 0)


def pick_columns(me_ref, grad_ref, *outs):
    width = outs[0].shape[1] // 2
    q = lax.rem(me_ref[0], grad_ref.shape[1] // width)
    for pair, out in enumerate(outs):
        for half in range(2):
            start = pl.multiple_of((q ^ (2 * pair + half)) * width, width)
            out[:, half * width : (half + 1) * width] = grad_ref[:, pl.ds(start, width)]


def stack_weight(own_ref, other_ref, out_ref):
    width = own_ref.shape[0]
    for tap in range(3):
        for part, ref in enumerate((own_ref, other_ref)):
            start = (2 * tap + part) * width
            out_ref[start : start + width, :] = ref[:, tap * C : (tap + 1) * C]


def routes(seg_count, chips, rows, me_ref, *refs):
    tables, source_ref, follow_ref = refs[:-2], refs[-2], refs[-1]
    slots = 2 * chips
    missing = slots * rows
    me = me_ref[0]
    for i in range(follow_ref.shape[0]):
        follow_ref[i] = missing
    for group in range(len(tables) // 2):
        for slot in range(slots):
            table = tables[2 * group + slot // chips]
            for position in range(seg_count):
                source = table[slot % chips, position]
                safe = jnp.maximum(source, 0)
                apart = (safe // seg_count) ^ me
                segment = ((apart & 1) * chips + (apart >> 1)) * seg_count + lax.rem(safe, seg_count)
                at = slot * seg_count + position
                source_ref[group * slots * seg_count + at] = jnp.where(source >= 0, segment * SEG, missing)

                @pl.when(source >= 0)
                def _():
                    follow_ref[group * slots * seg_count + segment] = at * SEG


def forward(own_class, me_ref, source_ref, weight_ref, *refs):
    blocks, (act_ref, sent_ref, rows_ref, early_ref) = refs[:-4], refs[-4:]
    count = blocks[0].shape[0]
    for i, block in enumerate(blocks):
        rows_ref[i * count : (i + 1) * count, :] = block[...]
    total = len(blocks) * count
    wide = weight_ref.shape[0] // 3
    nt = (((1,), (1,)), ((), ()))
    early_ref[:total, :] = lax.dot_general(
        rows_ref[...], weight_ref[: 2 * wide, :], nt, preferred_element_type=F32
    )
    early_ref[total:, :] = jnp.zeros((SEG, 2 * wide), F32)
    act_ref[...] = lax.dot_general(
        rows_ref[:own_class, :], weight_ref[2 * wide :, :], nt, preferred_element_type=F32
    )
    is_filter = me_ref[0] < me_ref[1]
    for segment in range(own_class // SEG):
        at = segment * SEG
        source = pl.multiple_of(source_ref[segment], SEG)
        carried = early_ref[pl.ds(source, SEG), :]
        preact = (
            act_ref[at : at + SEG, :]
            + carried[:, :wide]
            + roll_half(carried[:, wide:], early_ref[at : at + SEG, wide:])
        )
        act_ref[at : at + SEG, :] = jnp.where(is_filter, jnp.tanh(preact), jax.nn.sigmoid(preact))
    sent_ref[...] = act_ref[...].astype(BF16)


def gate(me_ref, act_ref, other_ref, *refs):
    grads, outs, pre_ref = refs[: len(refs) // 3 * 2], refs[len(refs) // 3 * 2 : -1], refs[-1]
    count = grads[0].shape[0]
    is_filter = me_ref[0] < me_ref[1]
    slots = len(grads)
    for slot, grad in enumerate(grads):
        at = slot * count
        there = (slot ^ (slots // 2)) * count
        mine = act_ref[at : at + count, :]
        theirs = other_ref[there : there + count, :].astype(F32)
        upstream = grad[...].astype(F32)
        if slot < len(outs):
            outs[slot][...] = (mine * theirs).astype(BF16)
        for_filter = upstream * theirs * (1.0 - mine * mine)
        for_gate = upstream * theirs * mine * (1.0 - mine)
        pre_ref[at : at + count, :] = jnp.where(is_filter, for_filter, for_gate).astype(BF16)


def input_grad(follow_ref, own_ref, other_ref, weight_ref, *refs):
    kept_ref, sends, sent_pre_ref, pre_ref, routed_ref = refs[0], refs[1:-3], refs[-3], refs[-2], refs[-1]
    total, wide = own_ref.shape
    width = wide // 2
    sent_pre_ref[:total, :] = own_ref[:, :width]
    sent_pre_ref[total:, :] = other_ref[:, width:]
    pre_ref[:total, :] = own_ref[...].astype(F32)
    pre_ref[total : 2 * total, :width] = other_ref[:, width:].astype(F32)
    pre_ref[total : 2 * total, width:] = other_ref[:, :width].astype(F32)
    pre_ref[2 * total :, :] = jnp.zeros((SEG, wide), F32)
    for segment in range(total // SEG):
        at = segment * SEG
        follow = pl.multiple_of(follow_ref[segment], SEG)
        carried = pre_ref[pl.ds(follow, SEG), :]
        local = pre_ref[at : at + SEG, :]
        routed_ref[at : at + SEG, :wide] = carried
        routed_ref[at : at + SEG, wide : 2 * wide] = roll_half(local, carried)
        routed_ref[at : at + SEG, 2 * wide :] = local
    part = jnp.dot(routed_ref[...].astype(BF16), weight_ref[...], preferred_element_type=F32)
    count = kept_ref.shape[0]
    kept_ref[...] = part[:count, :]
    for slot, out in enumerate(sends):
        out[...] = part[(slot + 1) * count : (slot + 2) * count, :].astype(BF16)


def weight_grad(groups, scale, follow_ref, *refs):
    per_group = (len(refs) - 4) // groups
    first_ref, out_ref, pre_ref, routed_ref, rows_ref = (None,) + refs[-4:]
    if (len(refs) - 4) % groups:
        first_ref, refs = refs[0], refs[1:]
        per_group = (len(refs) - 4) // groups
    total = pre_ref.shape[0] - SEG
    width = pre_ref.shape[1]
    pre_ref[total:, :] = jnp.zeros((SEG, width), F32)
    for group in range(groups):
        inputs = refs[group * per_group : (group + 1) * per_group]
        pre_ref[:total, :] = inputs[0][...].astype(F32)
        base = group * total
        at = base
        for block in inputs[1:]:
            rows_ref[at : at + block.shape[0], :] = block[...]
            at += block.shape[0]
        for segment in range(total // SEG):
            at = segment * SEG
            follow = pl.multiple_of(follow_ref[group * (total // SEG) + segment], SEG)
            carried = pre_ref[pl.ds(follow, SEG), :]
            local = pre_ref[at : at + SEG, :]
            at += base
            routed_ref[at : at + SEG, :width] = carried
            routed_ref[at : at + SEG, width : 2 * width] = roll_half(local, carried)
            routed_ref[at : at + SEG, 2 * width :] = local
    product = lax.dot_general(
        routed_ref[...].astype(BF16), rows_ref[...], (((0,), (0,)), ((), ())), preferred_element_type=F32
    )
    for tap in range(3):
        here = slice(tap * C, (tap + 1) * C)
        value = product[tap * width : (tap + 1) * width, :]
        if first_ref is not None:
            value = (value + first_ref[:, here]) * scale
        out_ref[:, here] = value


def place_gated(me_ref, *refs):
    pieces, out_ref = refs[:-1], refs[-1]
    width = pieces[0].shape[1] // 2
    q = lax.rem(me_ref[0], out_ref.shape[1] // width)
    for pair, piece in enumerate(pieces):
        for half in range(2):
            start = pl.multiple_of((q ^ (2 * pair + half)) * width, width)
            out_ref[:, pl.ds(start, width)] = piece[:, half * width : (half + 1) * width]


def add_parts(kept_ref, *refs):
    total = kept_ref[...]
    for part in refs[:-1]:
        total = total + part[...].astype(F32)
    refs[-1][...] = total.astype(BF16)


def by_channels(signal, grad_gated, conv_weight, source_seg):
    peers, groups = lax.axis_size("fsdp"), lax.axis_size("dp")
    chips = peers // 2
    seg_count = source_seg.shape[1]
    rows, width = signal.shape[0], conv_weight.shape[0]
    own_class, all_rows = chips * rows, peers * rows
    wide = 2 * width
    half_chips = chips // 2
    me = lax.axis_index("fsdp").astype(jnp.int32)
    who = jnp.stack([me, jnp.int32(peers // 2)])

    own_rows = [signal] + [swap(signal, "fsdp", 2 * k) for k in range(1, chips)]
    other_weight = swap(conv_weight, "fsdp", 1)
    tables = [jnp.concatenate([source_seg] + [swap(source_seg, "fsdp", 2 * k) for k in range(1, chips)], 0)]
    tables.append(swap(tables[0], "fsdp", 1))
    picked = call(
        pick_columns, [shaped((rows, wide), BF16)] * half_chips, [SMEM, VMEM]
    )(who, grad_gated)
    grads = [picked[0]] + [swap(picked[k % half_chips], "fsdp", 2 * k) for k in range(1, chips)]
    weight = call(stack_weight, [shaped((3 * wide, C), BF16)], [VMEM, VMEM])(conv_weight, other_weight)[0]
    other_rows = [swap(block, "fsdp", 1) for block in own_rows]

    def find_routes(*found):
        count = len(found) // 2 * peers * seg_count
        return call(
            functools.partial(routes, seg_count, chips, rows),
            [shaped((count,), jnp.int32)] * 2,
            [SMEM] * (1 + len(found)),
            out_specs=[SMEM] * 2,
        )(who, *found)

    sources, follows = find_routes(*tables)

    act, sent = call(
        functools.partial(forward, own_class),
        [shaped((own_class, wide), F32), shaped((own_class, wide), BF16)],
        [SMEM, SMEM] + [VMEM] * (1 + peers),
        [pltpu.VMEM((all_rows, C), BF16), pltpu.VMEM((all_rows + SEG, 2 * wide), F32)],
        flops=2 * all_rows * C * 3 * wide,
        moved=2 * all_rows * C,
    )(who, sources, weight, *own_rows, *other_rows)
    partner = swap(sent, "fsdp", peers // 2)

    far = []
    own_stack = jnp.concatenate(own_rows, 0)
    for d in range(1, groups):
        there = swap(own_stack, "dp", d)
        far.append([there, swap(there, "fsdp", 1)])
    far_tables = []
    for d in range(1, groups):
        far_tables += [swap(table, "dp", d) for table in tables]
    far_follows = find_routes(*far_tables)[1]

    *gated, pre = call(
        gate,
        [shaped((rows, wide), BF16)] * half_chips + [shaped((own_class, wide), BF16)],
        [SMEM] + [VMEM] * (2 + chips),
    )(who, act, partner, *grads)
    other_pre = swap(pre, "fsdp", 1)
    kept, *sends, sent_pre = call(
        input_grad,
        [shaped((rows, C), F32)] + [shaped((rows, C), BF16)] * (chips - 1) + [shaped((all_rows, width), BF16)],
        [SMEM, VMEM, VMEM, VMEM],
        [pltpu.VMEM((all_rows + SEG, wide), F32), pltpu.VMEM((own_class, 3 * wide), F32)],
        flops=2 * own_class * C * 3 * wide,
    )(follows, pre, other_pre, weight)
    parts = [swap(part, "fsdp", 2 * (k + 1)) for k, part in enumerate(sends)]
    far_pre = [swap(sent_pre, "dp", d) for d in range(1, groups)]
    gated = [gated[0]] + [swap(piece, "fsdp", 2 * (k + 1)) for k, piece in enumerate(gated[1:])]
    gated_out = call(place_gated, [shaped((rows, H), BF16)], [SMEM] + [VMEM] * len(gated))(who, *gated)[0]

    def grads_of(count, inputs, table, first):
        return call(
            functools.partial(weight_grad, count, 1.0 / math.sqrt(all_rows * groups)),
            [shaped((width, 3 * C), F32)],
            [SMEM] + [VMEM] * (len(inputs) + len(first)),
            [
                pltpu.VMEM((all_rows + SEG, width), F32),
                pltpu.VMEM((count * all_rows, 3 * width), F32),
                pltpu.VMEM((count * all_rows, C), BF16),
            ],
            flops=2 * count * all_rows * C * 3 * width,
        )(table, *first, *inputs)[0]

    near = grads_of(1, [sent_pre, *own_rows, *other_rows], follows, [])
    far_inputs = []
    for d in range(groups - 1):
        far_inputs += [far_pre[d], *far[d]]
    grad_weight = grads_of(groups - 1, far_inputs, far_follows, [near])
    grad_in = call(add_parts, [shaped((rows, C), BF16)], [VMEM] * chips)(kept, *parts)[0]
    return gated_out, grad_in, grad_weight


def tap_starts(context_row_block):
    return [context_row_block - (2 - selected_index) * DILATION_SIZE for selected_index in range(3)]


def by_rows(signal, grad_gated, conv_weight, source_seg):
    peer_count = lax.axis_size("fsdp")
    seg_count = source_seg.shape[1]
    row_count = signal.shape[0]
    seg_rows = row_count // seg_count
    context_row_block = 2 * DILATION_SIZE
    starts = tap_starts(context_row_block)
    segments = signal.reshape(seg_count, seg_rows, C)
    sources = source_seg[0]
    source_dev = jnp.where(sources >= 0, sources // seg_count, -1)
    peers = jnp.arange(peer_count, dtype=jnp.int32)
    request_mask = (source_dev[None, :] == peers[:, None]).astype(jnp.int32)
    asked = lax.all_to_all(request_mask, "fsdp", split_axis=0, concat_axis=0, tiled=True)
    send_table = asked.astype(jnp.bfloat16)
    recv_table = (source_dev[:, None] == peers[None, :]).astype(jnp.bfloat16)
    outgoing = jnp.einsum(
        "ns,slc->nlc", send_table, segments, preferred_element_type=jnp.float32
    ).astype(jnp.bfloat16)
    incoming = lax.all_to_all(outgoing, "fsdp", split_axis=0, concat_axis=0, tiled=True)
    carries = jnp.einsum(
        "sn,nlc->slc", recv_table, incoming, preferred_element_type=jnp.float32
    ).astype(jnp.bfloat16)
    extended = jnp.concatenate([carries, segments], axis=1)
    full_weight = lax.all_gather(conv_weight, "fsdp", axis=0, tiled=True)
    contract_final_axis = (((1,), (1,)), ((), ()))
    contract_first = (((0,), (0,)), ((), ()))
    windows = [extended[:, start : start + seg_rows, :].reshape(row_count, C) for start in starts]
    preact = sum(
        (
            lax.dot_general(
                windows[selected_index],
                full_weight[:, selected_index * C : (selected_index + 1) * C],
                contract_final_axis,
                preferred_element_type=jnp.float32,
            )
            for selected_index in range(3)
        )
    )
    filter_act = jnp.tanh(preact[:, :H])
    gate_act = jax.nn.sigmoid(preact[:, H:])
    gated_out = (filter_act * gate_act).astype(jnp.bfloat16)
    upstream_wide = grad_gated.astype(jnp.float32)
    grad_pre = jnp.concatenate(
        [
            upstream_wide * gate_act * (1.0 - filter_act * filter_act),
            upstream_wide * filter_act * gate_act * (1.0 - gate_act),
        ],
        axis=1,
    ).astype(jnp.bfloat16)
    partial_value = jnp.concatenate(
        [
            lax.dot_general(
                grad_pre,
                windows[selected_index],
                contract_first,
                preferred_element_type=jnp.float32,
            ).astype(jnp.bfloat16)
            for selected_index in range(3)
        ],
        axis=1,
    )
    arrived = lax.all_to_all(partial_value, "fsdp", split_axis=0, concat_axis=0, tiled=True)
    shard_sum = jnp.sum(arrived.reshape(peer_count, -1, 3 * C), axis=0, dtype=jnp.float32)
    group_total = lax.psum(shard_sum, "dp")
    total_token_count = row_count * peer_count * lax.axis_size("dp")
    grad_weight = group_total * (1.0 / math.sqrt(total_token_count))
    back_proj = jnp.dot(grad_pre, full_weight, preferred_element_type=jnp.float32)
    back_proj = back_proj.reshape(seg_count, seg_rows, 3 * C)
    grad_ext = jnp.zeros((seg_count, context_row_block + seg_rows, C), jnp.float32)
    for selected_index, start in enumerate(starts):
        grad_ext = grad_ext.at[:, start : start + seg_rows, :].add(
            back_proj[:, :, selected_index * C : (selected_index + 1) * C]
        )
    outgoing_grad = jnp.einsum(
        "sn,slc->nlc",
        recv_table.astype(jnp.float32),
        grad_ext[:, :context_row_block, :],
        precision=lax.Precision.HIGHEST,
    )
    incoming_grad = lax.all_to_all(outgoing_grad, "fsdp", split_axis=0, concat_axis=0, tiled=True)
    tail_grad = jnp.einsum(
        "ns,nlc->slc",
        send_table.astype(jnp.float32),
        incoming_grad,
        precision=lax.Precision.HIGHEST,
    )
    grad_in = (
        grad_ext[:, context_row_block:, :].at[:, seg_rows - context_row_block :, :].add(tail_grad)
    )
    grad_in = grad_in.reshape(row_count, C).astype(jnp.bfloat16)
    return (gated_out, grad_in, grad_weight)


def per_device(signal, grad_gated, conv_weight, source_seg):
    peers, groups = lax.axis_size("fsdp"), lax.axis_size("dp")
    rows, seg_count = signal.shape[0], source_seg.shape[1]
    fits = (
        rows == SEG * seg_count
        and conv_weight.shape[0] % 128 == 0
        and peers & (peers - 1) == 0
        and groups & (groups - 1) == 0
        and peers >= 4
        and groups >= 2
        and groups * peers * rows <= 2048
    )
    plan = by_channels if fits else by_rows
    return plan(signal, grad_gated, conv_weight, source_seg)


def solution(mesh):
    placed = (
        P(("dp", "fsdp"), None),
        P(("dp", "fsdp"), None),
        P("fsdp", None),
        P(("dp", "fsdp"), None),
    )
    return jax.shard_map(
        per_device,
        mesh=mesh,
        in_specs=placed,
        out_specs=(P(("dp", "fsdp"), None), P(("dp", "fsdp"), None), P("fsdp", None)),
        check_vma=False,
    )
```

```python
import functools
import math

import jax
import jax.numpy as jnp
from jax import lax
from jax.experimental import pallas as pl
from jax.experimental.pallas import tpu as pltpu
from jax.sharding import PartitionSpec as P

C = 1024
H = 512
DILATION_SIZE = 4
SEG = 8
BF16 = jnp.bfloat16
F32 = jnp.float32
VMEM = pl.BlockSpec(memory_space=pltpu.VMEM)
SMEM = pl.BlockSpec(memory_space=pltpu.SMEM)
ANY = pl.BlockSpec(memory_space=pl.ANY)
HBM = pl.BlockSpec(memory_space=pltpu.HBM)


def swap(value, axis, distance):
    count = lax.axis_size(axis)
    return lax.ppermute(value, axis, [(i, i ^ distance) for i in range(count)])


def exchange(copies, axis):
    return lax.all_to_all(copies, axis, split_axis=0, concat_axis=0, tiled=True)


def call(body, out_shapes, inputs, specs, scratch=(), out_specs=None, after=(), work=2e10, room=12, name=""):
    def run(*refs):
        body(*refs[len(after) :])

    return pl.pallas_call(
        run,
        out_shape=out_shapes,
        in_specs=[ANY] * len(after) + list(specs),
        out_specs=out_specs if out_specs is not None else [VMEM] * len(out_shapes),
        scratch_shapes=list(scratch),
        compiler_params=pltpu.CompilerParams(vmem_limit_bytes=room * 1024 * 1024),
        cost_estimate=pl.CostEstimate(flops=int(work), bytes_accessed=0, transcendentals=0),
    )(*after, *inputs)


def shaped(shape, dtype):
    return jax.ShapeDtypeStruct(shape, dtype)


def roll_half(first, second):
    row = lax.broadcasted_iota(jnp.int32, first.shape, 0)
    return pltpu.roll(jnp.where(row >= 4, first, second), 4, 0)


def pick(me_ref, grad_ref, *outs):
    half = outs[0].shape[1] // 2
    q = lax.rem(me_ref[0], grad_ref.shape[1] // half)
    for pair, out in enumerate(outs):
        for part in range(2):
            start = pl.multiple_of((q ^ (2 * pair + part)) * half, half)
            out[:, part * half : (part + 1) * half] = grad_ref[:, pl.ds(start, half)]


def stack_weight(own_ref, other_ref, out_ref):
    width = own_ref.shape[0]
    for tap in range(3):
        for part, ref in enumerate((own_ref, other_ref)):
            start = (2 * tap + part) * width
            out_ref[start : start + width, :] = ref[:, tap * C : (tap + 1) * C]


def place(source, seg_count, chips, me):
    apart = (source // seg_count) ^ me
    return ((apart & 1) * chips + (apart >> 1)) * seg_count + lax.rem(source, seg_count)


def find_follows(chips, me, source, follow_ref, table):
    peers = 2 * chips
    segments = follow_ref.shape[1]
    seg_count = segments // peers
    for i in range(segments):
        follow_ref[table, i] = segments * SEG
    for peer in range(peers):
        slot = place(peer * seg_count, seg_count, chips, me)
        for position in range(seg_count):
            found = source(peer, position)

            @pl.when(found >= 0)
            def _():
                follow_ref[table, place(found, seg_count, chips, me)] = (slot + position) * SEG


def follows(chips, me_ref, table_ref, follow_ref):
    find_follows(chips, me_ref[0], lambda peer, position: table_ref[peer, position], follow_ref, 0)


def far_follows(chips, me_ref, *refs):
    blocks, (follow_ref, raw_ref, wide_ref, table_ref, sems) = refs[:-5], refs[-5:]
    count = len(blocks)
    seg_count = follow_ref.shape[1] // (2 * chips)
    loads = []
    for i, block in enumerate(blocks):
        rows = pl.ds(block.shape[0] - 16, 16)
        loads.append(pltpu.make_async_copy(block.at[rows, pl.ds(0, 128)], raw_ref.at[i], sems.at[i]))
        loads[-1].start()
    for load in loads:
        load.wait()
    wide_ref[...] = raw_ref[...].astype(F32).astype(jnp.int32)
    moved = pltpu.make_async_copy(wide_ref, table_ref, sems.at[0])
    moved.start()
    moved.wait()

    def one(table, carry):
        find_follows(
            chips,
            me_ref[0],
            lambda peer, position: table_ref[table, 0, peer * seg_count + position],
            follow_ref,
            table,
        )
        return carry

    lax.fori_loop(0, count, one, 0)


def stack(table_ref, *refs):
    blocks, (rows_ref, copy_ref) = refs[:-2], refs[-2:]
    count = blocks[0].shape[0]
    for slot, block in enumerate(blocks):
        rows_ref[slot * count : (slot + 1) * count, :] = block[...]
        copy_ref[slot * count : (slot + 1) * count, :] = block[...]
    peers, seg_count = table_ref.shape
    lane = lax.broadcasted_iota(jnp.int32, (16, 128), 1)
    value = jnp.zeros((16, 128), jnp.int32)
    for peer in range(peers):
        for position in range(seg_count):
            value = jnp.where(lane == peer * seg_count + position, table_ref[peer, position], value)
    total = rows_ref.shape[0]
    copy_ref[total:, :] = jnp.zeros((16, C), BF16)
    copy_ref[total:, :128] = value.astype(F32).astype(BF16)


def forward(me_ref, table_ref, weight_ref, own_ref, other_ref, grad_ref, act_ref, sent_ref, rows_ref, early_ref):
    own_class = own_ref.shape[0]
    peers, seg_count = table_ref.shape
    me = me_ref[0]
    rows_ref[:own_class, :] = own_ref[...]
    rows_ref[own_class:, :] = other_ref[...]
    total = 2 * own_class
    wide = weight_ref.shape[0] // 3
    nt = (((1,), (1,)), ((), ()))
    early_ref[:total, :] = lax.dot_general(
        rows_ref[...], weight_ref[: 2 * wide, :], nt, preferred_element_type=F32
    )
    early_ref[total:, :] = jnp.zeros((SEG, 2 * wide), F32)
    act_ref[...] = lax.dot_general(
        rows_ref[:own_class, :], weight_ref[2 * wide :, :], nt, preferred_element_type=F32
    )
    is_filter = me_ref[0] < me_ref[1]
    for segment in range(own_class // SEG):
        at = segment * SEG
        source = table_ref[me ^ (2 * (segment // seg_count)), segment % seg_count]
        found = place(jnp.maximum(source, 0), seg_count, peers // 2, me)
        source = pl.multiple_of(jnp.where(source >= 0, found * SEG, total), SEG)
        carried = early_ref[pl.ds(source, SEG), :]
        preact = (
            act_ref[at : at + SEG, :]
            + carried[:, :wide]
            + roll_half(carried[:, wide:], early_ref[at : at + SEG, wide:])
        )
        act_ref[at : at + SEG, :] = jnp.where(is_filter, jnp.tanh(preact), jax.nn.sigmoid(preact))
    sent_ref[:own_class, :] = act_ref[...].astype(BF16)
    sent_ref[own_class:, :] = grad_ref[...]


def gate(me_ref, act_ref, other_ref, *refs):
    grads, outs, pre_ref = list(refs[:-3]), refs[-3:-1], refs[-1]
    count = outs[0].shape[0]
    is_filter = me_ref[0] < me_ref[1]
    slots = len(grads) + 1
    grads.insert(slots // 2, other_ref.at[slots * count :, :])
    for slot, grad in enumerate(grads):
        at = slot * count
        there = (slot ^ (slots // 2)) * count
        mine = act_ref[at : at + count, :]
        theirs = other_ref[there : there + count, :].astype(F32)
        upstream = grad[...].astype(F32)
        if slot < len(outs):
            outs[slot][...] = (mine * theirs).astype(BF16)
        for_filter = upstream * theirs * (1.0 - mine * mine)
        for_gate = upstream * theirs * mine * (1.0 - mine)
        pre_ref[at : at + count, :] = jnp.where(is_filter, for_filter, for_gate).astype(BF16)


def input_grad(follow_ref, own_ref, other_ref, weight_ref, gated_ref, *refs):
    sends, here_ref, pre_ref, routed_ref = refs[:-3], refs[-3], refs[-2], refs[-1]
    total, wide = own_ref.shape
    width = wide // 2
    pre_ref[:total, :] = own_ref[...].astype(F32)
    pre_ref[total : 2 * total, :width] = other_ref[:, width:].astype(F32)
    pre_ref[total : 2 * total, width:] = other_ref[:, :width].astype(F32)
    pre_ref[2 * total :, :] = jnp.zeros((SEG, wide), F32)
    for segment in range(total // SEG):
        at = segment * SEG
        follow = pl.multiple_of(follow_ref[0, segment], SEG)
        carried = pre_ref[pl.ds(follow, SEG), :]
        local = pre_ref[at : at + SEG, :]
        routed_ref[at : at + SEG, :wide] = carried
        routed_ref[at : at + SEG, wide : 2 * wide] = roll_half(local, carried)
        routed_ref[at : at + SEG, 2 * wide :] = local
    count = here_ref.shape[0]
    fold = C // wide
    for i in range(fold):
        piece = gated_ref[i * (count // fold) : (i + 1) * (count // fold), :]
        sends[0][count:, i * wide : (i + 1) * wide] = piece
    routed = routed_ref[...].astype(BF16)
    here_ref[...] = routed[:count, :]
    part = jnp.dot(routed[count:, :], weight_ref[...], preferred_element_type=F32)
    for slot, out in enumerate(sends):
        out[:count, :] = part[slot * count : (slot + 1) * count, :].astype(BF16)


def spread(own_ref, other_ref, copies_ref):
    total, wide = own_ref.shape
    width = wide // 2
    for copy in range(copies_ref.shape[0]):
        copies_ref[copy, :total, :] = own_ref[:, :width]
        copies_ref[copy, total:, :] = other_ref[:, width:]


def nothing(*refs):
    pass


def held(values, after):
    return pl.pallas_call(
        nothing,
        out_shape=[shaped(value.shape, value.dtype) for value in values],
        in_specs=[ANY] * (len(values) + len(after)),
        out_specs=[ANY] * len(values),
        input_output_aliases={i: i for i in range(len(values))},
        compiler_params=pltpu.CompilerParams(vmem_limit_bytes=2**20),
        cost_estimate=pl.CostEstimate(flops=10**10, bytes_accessed=0, transcendentals=0),
    )(*values, *after)


def weight_grad(which, scale, group_ref, follow_ref, *refs):
    first_ref = refs[0] if len(which) > 1 else None
    sent_pre_ref = refs[-5 - 2 * len(which)]
    signals = refs[-4 - 2 * len(which) : -4]
    out_ref, pre_ref, routed_ref, rows_ref = refs[-4:]
    total = pre_ref.shape[0] - SEG
    width = pre_ref.shape[1]
    pre_ref[total:, :] = jnp.zeros((SEG, width), F32)
    for i, distance in enumerate(which):
        base = i * total
        pre_ref[:total, :] = sent_pre_ref[group_ref[0] ^ distance].astype(F32)
        rows_ref[base : base + total // 2, :] = signals[2 * i][: total // 2, :]
        rows_ref[base + total // 2 : base + total, :] = signals[2 * i + 1][: total // 2, :]
        for segment in range(total // SEG):
            at = segment * SEG
            follow = pl.multiple_of(follow_ref[i, segment], SEG)
            carried = pre_ref[pl.ds(follow, SEG), :]
            local = pre_ref[at : at + SEG, :]
            at += base
            routed_ref[at : at + SEG, :width] = carried
            routed_ref[at : at + SEG, width : 2 * width] = roll_half(local, carried)
            routed_ref[at : at + SEG, 2 * width :] = local
    product = lax.dot_general(
        routed_ref[...].astype(BF16), rows_ref[...], (((0,), (0,)), ((), ())), preferred_element_type=F32
    )
    for tap in range(3):
        here = slice(tap * C, (tap + 1) * C)
        value = product[tap * width : (tap + 1) * width, :]
        if first_ref is not None:
            value = (value + first_ref[:, here]) * scale
        out_ref[:, here] = value


def finish(me_ref, here_ref, weight_ref, gated_ref, *refs):
    parts, (grad_ref, out_ref) = refs[:-2], refs[-2:]
    count = grad_ref.shape[0]
    total = jnp.dot(here_ref[...], weight_ref[...], preferred_element_type=F32)
    for part in parts:
        total = total + part[:count, :].astype(F32)
    grad_ref[...] = total.astype(BF16)
    wide = gated_ref.shape[1]
    width = wide // 2
    fold = C // wide
    short = count // fold
    q = lax.rem(me_ref[0], out_ref.shape[1] // width)
    for part in range(2):
        here = slice(part * width, (part + 1) * width)
        out_ref[:, pl.ds(pl.multiple_of((q ^ part) * width, width), width)] = gated_ref[:, here]
        start = pl.multiple_of((q ^ (2 + part)) * width, width)
        for i in range(fold):
            piece = parts[0][count:, i * wide + part * width : i * wide + (part + 1) * width]
            out_ref[i * short : (i + 1) * short, pl.ds(start, width)] = piece


def by_channels(signal, grad_gated, conv_weight, source_seg):
    peers, groups = lax.axis_size("fsdp"), lax.axis_size("dp")
    chips = peers // 2
    seg_count = source_seg.shape[1]
    rows, width = signal.shape[0], conv_weight.shape[0]
    own_class, all_rows = chips * rows, peers * rows
    wide = 2 * width
    half_chips = chips // 2
    me = lax.axis_index("fsdp").astype(jnp.int32)
    group = lax.axis_index("dp").astype(jnp.int32)
    who = jnp.stack([me, jnp.int32(peers // 2)])

    fold = C // wide
    own_rows = [signal] + [swap(signal, "fsdp", 2 * k) for k in range(1, chips)]
    picked = call(
        pick, [shaped((rows, wide), BF16)] * half_chips, [who, grad_gated], [SMEM, VMEM], name="pick"
    )
    other_weight = swap(conv_weight, "fsdp", 1)
    weight = call(
        stack_weight, [shaped((3 * wide, C), BF16)], [conv_weight, other_weight], [VMEM] * 2, name="wstack"
    )[0]
    table = exchange(jnp.broadcast_to(source_seg[None], (peers, 1, seg_count)), "fsdp").reshape(peers, seg_count)
    own_stack, own_copy = call(
        stack,
        [shaped((own_class, C), BF16), shaped((own_class + 16, C), BF16)],
        [table, *own_rows],
        [SMEM] + [VMEM] * chips,
        name="stack",
    )
    other_stack = swap(own_stack, "fsdp", 1)
    act, sent = call(
        forward,
        [shaped((own_class, wide), F32), shaped((own_class + rows, wide), BF16)],
        [who, table, weight, own_stack, other_stack, picked[0]],
        [SMEM, SMEM] + [VMEM] * 4,
        [pltpu.VMEM((all_rows, C), BF16), pltpu.VMEM((all_rows + SEG, 2 * wide), F32)],
        name="forward",
    )
    partner = swap(sent, "fsdp", peers // 2)
    grads = [picked[0], swap(picked[1], "fsdp", 2), swap(picked[1], "fsdp", 6)]

    follow = call(
        functools.partial(follows, chips),
        [shaped((1, peers * seg_count), jnp.int32)],
        [who, table],
        [SMEM, SMEM],
        out_specs=[SMEM],
        after=[sent],
        name="follow",
    )[0]
    far_own = [swap(own_copy, "dp", d) for d in (1, 2)]
    *far_own, own_copy = held([*far_own, own_copy], [follow])
    last_own = swap(own_copy, "dp", 3)
    far_other = [swap(block, "fsdp", 1) for block in far_own]

    *gated, pre = call(
        gate,
        [shaped((rows, wide), BF16)] * half_chips + [shaped((own_class, wide), BF16)],
        [who, act, partner, *grads],
        [SMEM] + [VMEM] * (2 + len(grads)),
        after=[own_copy],
        name="gate",
    )
    other_pre = swap(pre, "fsdp", 1)
    *sends, here = call(
        input_grad,
        [shaped((rows + rows // fold, C), BF16)]
        + [shaped((rows, C), BF16)] * (chips - 2)
        + [shaped((rows, 3 * wide), BF16)],
        [follow, pre, other_pre, weight, gated[1]],
        [SMEM, VMEM, VMEM, VMEM, VMEM],
        [pltpu.VMEM((all_rows + SEG, wide), F32), pltpu.VMEM((own_class, 3 * wide), F32)],
        after=far_other,
        name="input",
    )
    parts = [swap(part, "fsdp", 2 * (k + 1)) for k, part in enumerate(sends)]
    sent_pre = call(
        spread, [shaped((groups, all_rows, width), BF16)], [pre, other_pre], [VMEM] * 2, after=[here], name="spread"
    )[0]
    far_pre = exchange(sent_pre, "dp")

    def grads_of(which, found, inputs, first, name):
        count = len(which)
        return call(
            functools.partial(weight_grad, which, 1.0 / math.sqrt(all_rows * groups)),
            [shaped((width, 3 * C), F32)],
            [group[None], found, *first, *inputs],
            [SMEM, SMEM] + [VMEM] * (len(inputs) + len(first)),
            [
                pltpu.VMEM((all_rows + SEG, width), F32),
                pltpu.VMEM((count * all_rows, 3 * width), F32),
                pltpu.VMEM((count * all_rows, C), BF16),
            ],
            room=24,
            name=name,
        )[0]

    near = grads_of([0], follow, [sent_pre, own_stack, other_stack], [], "near")
    last_own = held([last_own], [near])[0]
    far_own.append(last_own)
    far_other.append(swap(last_own, "fsdp", 1))
    far_follow = call(
        functools.partial(far_follows, chips),
        [shaped((groups - 1, peers * seg_count), jnp.int32)],
        [who, *far_own],
        [SMEM] + [ANY] * len(far_own),
        [
            pltpu.VMEM((groups - 1, 16, 128), BF16),
            pltpu.VMEM((groups - 1, 16, 128), jnp.int32),
            pltpu.SMEM((groups - 1, 16, 128), jnp.int32),
            pltpu.SemaphoreType.DMA((groups - 1,)),
        ],
        out_specs=[SMEM],
        name="farfollow",
    )[0]
    grad_in, gated_out = call(
        finish,
        [shaped((rows, C), BF16), shaped((rows, H), BF16)],
        [who, here, weight, gated[0], *parts],
        [SMEM] + [VMEM] * (chips + 2),
        name="finish",
    )
    far_signals = [block for pair in zip(far_own, far_other) for block in pair]
    grad_weight = grads_of(list(range(1, groups)), far_follow, [far_pre, *far_signals], [near], "far")
    return gated_out, grad_in, grad_weight


def tap_starts(context_row_block):
    return [context_row_block - (2 - selected_index) * DILATION_SIZE for selected_index in range(3)]


def by_rows(signal, grad_gated, conv_weight, source_seg):
    peer_count = lax.axis_size("fsdp")
    seg_count = source_seg.shape[1]
    row_count = signal.shape[0]
    seg_rows = row_count // seg_count
    context_row_block = 2 * DILATION_SIZE
    starts = tap_starts(context_row_block)
    segments = signal.reshape(seg_count, seg_rows, C)
    sources = source_seg[0]
    source_dev = jnp.where(sources >= 0, sources // seg_count, -1)
    peers = jnp.arange(peer_count, dtype=jnp.int32)
    request_mask = (source_dev[None, :] == peers[:, None]).astype(jnp.int32)
    asked = lax.all_to_all(request_mask, "fsdp", split_axis=0, concat_axis=0, tiled=True)
    send_table = asked.astype(jnp.bfloat16)
    recv_table = (source_dev[:, None] == peers[None, :]).astype(jnp.bfloat16)
    outgoing = jnp.einsum(
        "ns,slc->nlc", send_table, segments, preferred_element_type=jnp.float32
    ).astype(jnp.bfloat16)
    incoming = lax.all_to_all(outgoing, "fsdp", split_axis=0, concat_axis=0, tiled=True)
    carries = jnp.einsum(
        "sn,nlc->slc", recv_table, incoming, preferred_element_type=jnp.float32
    ).astype(jnp.bfloat16)
    extended = jnp.concatenate([carries, segments], axis=1)
    full_weight = lax.all_gather(conv_weight, "fsdp", axis=0, tiled=True)
    contract_final_axis = (((1,), (1,)), ((), ()))
    contract_first = (((0,), (0,)), ((), ()))
    windows = [extended[:, start : start + seg_rows, :].reshape(row_count, C) for start in starts]
    preact = sum(
        (
            lax.dot_general(
                windows[selected_index],
                full_weight[:, selected_index * C : (selected_index + 1) * C],
                contract_final_axis,
                preferred_element_type=jnp.float32,
            )
            for selected_index in range(3)
        )
    )
    filter_act = jnp.tanh(preact[:, :H])
    gate_act = jax.nn.sigmoid(preact[:, H:])
    gated_out = (filter_act * gate_act).astype(jnp.bfloat16)
    upstream_wide = grad_gated.astype(jnp.float32)
    grad_pre = jnp.concatenate(
        [
            upstream_wide * gate_act * (1.0 - filter_act * filter_act),
            upstream_wide * filter_act * gate_act * (1.0 - gate_act),
        ],
        axis=1,
    ).astype(jnp.bfloat16)
    partial_value = jnp.concatenate(
        [
            lax.dot_general(
                grad_pre,
                windows[selected_index],
                contract_first,
                preferred_element_type=jnp.float32,
            ).astype(jnp.bfloat16)
            for selected_index in range(3)
        ],
        axis=1,
    )
    arrived = lax.all_to_all(partial_value, "fsdp", split_axis=0, concat_axis=0, tiled=True)
    shard_sum = jnp.sum(arrived.reshape(peer_count, -1, 3 * C), axis=0, dtype=jnp.float32)
    group_total = lax.psum(shard_sum, "dp")
    total_token_count = row_count * peer_count * lax.axis_size("dp")
    grad_weight = group_total * (1.0 / math.sqrt(total_token_count))
    back_proj = jnp.dot(grad_pre, full_weight, preferred_element_type=jnp.float32)
    back_proj = back_proj.reshape(seg_count, seg_rows, 3 * C)
    grad_ext = jnp.zeros((seg_count, context_row_block + seg_rows, C), jnp.float32)
    for selected_index, start in enumerate(starts):
        grad_ext = grad_ext.at[:, start : start + seg_rows, :].add(
            back_proj[:, :, selected_index * C : (selected_index + 1) * C]
        )
    outgoing_grad = jnp.einsum(
        "sn,slc->nlc",
        recv_table.astype(jnp.float32),
        grad_ext[:, :context_row_block, :],
        precision=lax.Precision.HIGHEST,
    )
    incoming_grad = lax.all_to_all(outgoing_grad, "fsdp", split_axis=0, concat_axis=0, tiled=True)
    tail_grad = jnp.einsum(
        "ns,nlc->slc",
        send_table.astype(jnp.float32),
        incoming_grad,
        precision=lax.Precision.HIGHEST,
    )
    grad_in = (
        grad_ext[:, context_row_block:, :].at[:, seg_rows - context_row_block :, :].add(tail_grad)
    )
    grad_in = grad_in.reshape(row_count, C).astype(jnp.bfloat16)
    return (gated_out, grad_in, grad_weight)


def per_device(signal, grad_gated, conv_weight, source_seg):
    peers, groups = lax.axis_size("fsdp"), lax.axis_size("dp")
    rows, seg_count = signal.shape[0], source_seg.shape[1]
    fits = (
        rows == SEG * seg_count
        and conv_weight.shape[0] % 128 == 0
        and peers & (peers - 1) == 0
        and groups & (groups - 1) == 0
        and peers == 8
        and groups == 4
        and groups * peers * rows <= 2048
        and rows % 64 == 0
        and peers * seg_count <= 128
    )
    plan = by_channels if fits else by_rows
    return plan(signal, grad_gated, conv_weight, source_seg)


def solution(mesh):
    placed = (
        P(("dp", "fsdp"), None),
        P(("dp", "fsdp"), None),
        P("fsdp", None),
        P(("dp", "fsdp"), None),
    )
    return jax.shard_map(
        per_device,
        mesh=mesh,
        in_specs=placed,
        out_specs=(P(("dp", "fsdp"), None), P(("dp", "fsdp"), None), P("fsdp", None)),
        check_vma=False,
    )
```

```python
import functools
import math

import jax
import jax.numpy as jnp
from jax import lax
from jax.experimental import pallas as pl
from jax.experimental.pallas import tpu as pltpu
from jax.sharding import PartitionSpec as P

C = 1024
H = 512
DILATION_SIZE = 4
SEG = 8
BF16 = jnp.bfloat16
F32 = jnp.float32
VMEM = pl.BlockSpec(memory_space=pltpu.VMEM)
SMEM = pl.BlockSpec(memory_space=pltpu.SMEM)
ANY = pl.BlockSpec(memory_space=pl.ANY)
HBM = pl.BlockSpec(memory_space=pltpu.HBM)


def swap(value, axis, distance):
    count = lax.axis_size(axis)
    return lax.ppermute(value, axis, [(i, i ^ distance) for i in range(count)])


def exchange(copies, axis):
    return lax.all_to_all(copies, axis, split_axis=0, concat_axis=0, tiled=True)


def call(body, out_shapes, inputs, specs, scratch=(), out_specs=None, after=(), work=1e10, room=12):
    def run(*refs):
        body(*refs[len(after) :])

    return pl.pallas_call(
        run,
        out_shape=out_shapes,
        in_specs=[ANY] * len(after) + list(specs),
        out_specs=out_specs if out_specs is not None else [VMEM] * len(out_shapes),
        scratch_shapes=list(scratch),
        compiler_params=pltpu.CompilerParams(vmem_limit_bytes=room * 1024 * 1024),
        cost_estimate=pl.CostEstimate(flops=int(work), bytes_accessed=0, transcendentals=0),
    )(*after, *inputs)


def shaped(shape, dtype):
    return jax.ShapeDtypeStruct(shape, dtype)


def roll_half(first, second):
    row = lax.broadcasted_iota(jnp.int32, first.shape, 0)
    return pltpu.roll(jnp.where(row >= 4, first, second), 4, 0)


def pick(me_ref, grad_ref, *outs):
    half = outs[0].shape[1] // 2
    q = lax.rem(me_ref[0], grad_ref.shape[1] // half)
    for pair, out in enumerate(outs):
        for part in range(2):
            start = pl.multiple_of((q ^ (2 * pair + part)) * half, half)
            out[:, part * half : (part + 1) * half] = grad_ref[:, pl.ds(start, half)]


def stack_weight(own_ref, other_ref, out_ref):
    width = own_ref.shape[0]
    for tap in range(3):
        for part, ref in enumerate((own_ref, other_ref)):
            start = (2 * tap + part) * width
            out_ref[start : start + width, :] = ref[:, tap * C : (tap + 1) * C]


def place(source, seg_count, chips, me):
    apart = (source // seg_count) ^ me
    return ((apart & 1) * chips + (apart >> 1)) * seg_count + lax.rem(source, seg_count)


def follows(chips, me_ref, table_ref, follow_ref):
    peers, seg_count = table_ref.shape
    me = me_ref[0]
    for i in range(peers * seg_count):
        follow_ref[i] = peers * seg_count
    for peer in range(peers):
        slot = place(peer * seg_count, seg_count, chips, me)
        for position in range(seg_count):
            source = table_ref[peer, position]

            @pl.when(source >= 0)
            def _():
                follow_ref[place(source, seg_count, chips, me)] = slot + position


def stack(*refs):
    blocks, out_ref = refs[:-1], refs[-1]
    count = blocks[0].shape[0]
    for slot, block in enumerate(blocks):
        out_ref[slot * count : (slot + 1) * count, :] = block[...]


def forward(me_ref, table_ref, weight_ref, own_ref, other_ref, grad_ref, act_ref, sent_ref, rows_ref, early_ref):
    own_class = own_ref.shape[0]
    peers, seg_count = table_ref.shape
    me = me_ref[0]
    rows_ref[:own_class, :] = own_ref[...]
    rows_ref[own_class:, :] = other_ref[...]
    total = 2 * own_class
    wide = weight_ref.shape[0] // 3
    nt = (((1,), (1,)), ((), ()))
    early_ref[:total, :] = lax.dot_general(
        rows_ref[...], weight_ref[: 2 * wide, :], nt, preferred_element_type=F32
    )
    early_ref[total:, :] = jnp.zeros((SEG, 2 * wide), F32)
    act_ref[...] = lax.dot_general(
        rows_ref[:own_class, :], weight_ref[2 * wide :, :], nt, preferred_element_type=F32
    )
    is_filter = me_ref[0] < me_ref[1]
    for segment in range(own_class // SEG):
        at = segment * SEG
        source = table_ref[me ^ (2 * (segment // seg_count)), segment % seg_count]
        found = place(jnp.maximum(source, 0), seg_count, peers // 2, me)
        source = pl.multiple_of(jnp.where(source >= 0, found * SEG, total), SEG)
        carried = early_ref[pl.ds(source, SEG), :]
        preact = (
            act_ref[at : at + SEG, :]
            + carried[:, :wide]
            + roll_half(carried[:, wide:], early_ref[at : at + SEG, wide:])
        )
        act_ref[at : at + SEG, :] = jnp.where(is_filter, jnp.tanh(preact), jax.nn.sigmoid(preact))
    sent_ref[:own_class, :] = act_ref[...].astype(BF16)
    sent_ref[own_class:, :] = grad_ref[...]


def gate(me_ref, act_ref, other_ref, *refs):
    grads, outs, pre_ref = list(refs[:-3]), refs[-3:-1], refs[-1]
    count = outs[0].shape[0]
    is_filter = me_ref[0] < me_ref[1]
    slots = len(grads) + 1
    grads.insert(slots // 2, other_ref.at[slots * count :, :])
    for slot, grad in enumerate(grads):
        at = slot * count
        there = (slot ^ (slots // 2)) * count
        mine = act_ref[at : at + count, :]
        theirs = other_ref[there : there + count, :].astype(F32)
        upstream = grad[...].astype(F32)
        if slot < len(outs):
            outs[slot][...] = (mine * theirs).astype(BF16)
        for_filter = upstream * theirs * (1.0 - mine * mine)
        for_gate = upstream * theirs * mine * (1.0 - mine)
        pre_ref[at : at + count, :] = jnp.where(is_filter, for_filter, for_gate).astype(BF16)


def input_grad(follow_ref, own_ref, other_ref, weight_ref, gated_ref, *refs):
    sends, here_ref, pre_ref, routed_ref = refs[:-3], refs[-3], refs[-2], refs[-1]
    total, wide = own_ref.shape
    width = wide // 2
    pre_ref[:total, :] = own_ref[...].astype(F32)
    pre_ref[total : 2 * total, :width] = other_ref[:, width:].astype(F32)
    pre_ref[total : 2 * total, width:] = other_ref[:, :width].astype(F32)
    pre_ref[2 * total :, :] = jnp.zeros((SEG, wide), F32)
    for segment in range(total // SEG):
        at = segment * SEG
        follow = pl.multiple_of(follow_ref[segment] * SEG, SEG)
        carried = pre_ref[pl.ds(follow, SEG), :]
        local = pre_ref[at : at + SEG, :]
        routed_ref[at : at + SEG, :wide] = carried
        routed_ref[at : at + SEG, wide : 2 * wide] = roll_half(local, carried)
        routed_ref[at : at + SEG, 2 * wide :] = local
    count = here_ref.shape[0]
    fold = C // wide
    for i in range(fold):
        piece = gated_ref[i * (count // fold) : (i + 1) * (count // fold), :]
        sends[0][count:, i * wide : (i + 1) * wide] = piece
    routed = routed_ref[...].astype(BF16)
    here_ref[...] = routed[:count, :]
    part = jnp.dot(routed[count:, :], weight_ref[...], preferred_element_type=F32)
    for slot, out in enumerate(sends):
        out[:count, :] = part[slot * count : (slot + 1) * count, :].astype(BF16)


def spread(follow_ref, own_ref, other_ref, copies_ref):
    total, wide = own_ref.shape
    width = wide // 2
    lane = lax.broadcasted_iota(jnp.int32, (16, width), 1)
    value = jnp.zeros((16, width), jnp.int32)
    for segment in range(follow_ref.shape[0]):
        value = jnp.where(lane == segment, follow_ref[segment], value)
    value = value.astype(F32).astype(BF16)
    for copy in range(copies_ref.shape[0]):
        copies_ref[copy, :total, :] = own_ref[:, :width]
        copies_ref[copy, total : 2 * total, :] = other_ref[:, width:]
        copies_ref[copy, 2 * total :, :] = value


def local(here_ref, weight_ref, out_ref):
    out_ref[...] = jnp.dot(here_ref[...], weight_ref[...], preferred_element_type=F32)


def mark(out_ref):
    out_ref[...] = jnp.zeros(out_ref.shape, out_ref.dtype)


def nothing(*refs):
    pass


def held(values, after):
    return pl.pallas_call(
        nothing,
        out_shape=[shaped(value.shape, value.dtype) for value in values],
        in_specs=[ANY] * (len(values) + len(after)),
        out_specs=[ANY] * len(values),
        input_output_aliases={i: i for i in range(len(values))},
        compiler_params=pltpu.CompilerParams(vmem_limit_bytes=2**20),
        cost_estimate=pl.CostEstimate(flops=10000000, bytes_accessed=0, transcendentals=0),
    )(*values, *after)


def weight_grad(scale, group_ref, pre_ref, *refs):
    blocks = refs[:-7]
    out_ref, early_ref, routed_ref, rows_ref, wide_ref, follow_ref, sem = refs[-7:]
    groups, total, width = early_ref.shape
    total -= SEG
    for i in range(groups):
        wide_ref[i] = pre_ref[group_ref[0] ^ i, total:, :].astype(F32).astype(jnp.int32)
    load = pltpu.make_async_copy(wide_ref, follow_ref, sem)
    load.start()
    for i, block in enumerate(blocks):
        count = block.shape[0]
        rows_ref[i * count : (i + 1) * count, :] = block[...]
    for i in range(groups):
        early_ref[i, :total, :] = pre_ref[group_ref[0] ^ i, :total, :].astype(F32)
        early_ref[i, total:, :] = jnp.zeros((SEG, width), F32)
    load.wait()
    for i in range(groups):
        for segment in range(total // SEG):
            at = segment * SEG
            follow = pl.multiple_of(follow_ref[i, 0, segment] * SEG, SEG)
            carried = early_ref[i, pl.ds(follow, SEG), :]
            local = early_ref[i, at : at + SEG, :]
            at += i * total
            routed_ref[at : at + SEG, :width] = carried
            routed_ref[at : at + SEG, width : 2 * width] = roll_half(local, carried)
            routed_ref[at : at + SEG, 2 * width :] = local
    product = lax.dot_general(
        routed_ref[...].astype(BF16), rows_ref[...], (((0,), (0,)), ((), ())), preferred_element_type=F32
    )
    for tap in range(3):
        out_ref[:, tap * C : (tap + 1) * C] = product[tap * width : (tap + 1) * width, :] * scale


def finish(me_ref, kept_ref, gated_ref, *refs):
    parts, (grad_ref, out_ref) = refs[:-2], refs[-2:]
    count = grad_ref.shape[0]
    total = kept_ref[...]
    for part in parts:
        total = total + part[:count, :].astype(F32)
    grad_ref[...] = total.astype(BF16)
    wide = gated_ref.shape[1]
    width = wide // 2
    fold = C // wide
    short = count // fold
    q = lax.rem(me_ref[0], out_ref.shape[1] // width)
    for part in range(2):
        here = slice(part * width, (part + 1) * width)
        out_ref[:, pl.ds(pl.multiple_of((q ^ part) * width, width), width)] = gated_ref[:, here]
        start = pl.multiple_of((q ^ (2 + part)) * width, width)
        for i in range(fold):
            piece = parts[0][count:, i * wide + part * width : i * wide + (part + 1) * width]
            out_ref[i * short : (i + 1) * short, pl.ds(start, width)] = piece


def by_channels(signal, grad_gated, conv_weight, source_seg):
    peers, groups = lax.axis_size("fsdp"), lax.axis_size("dp")
    chips = peers // 2
    seg_count = source_seg.shape[1]
    rows, width = signal.shape[0], conv_weight.shape[0]
    own_class, all_rows = chips * rows, peers * rows
    wide = 2 * width
    half_chips = chips // 2
    me = lax.axis_index("fsdp").astype(jnp.int32)
    group = lax.axis_index("dp").astype(jnp.int32)
    who = jnp.stack([me, jnp.int32(peers // 2)])

    fold = C // wide
    own_rows = [signal] + [swap(signal, "fsdp", 2 * k) for k in range(1, chips)]
    picked = call(
        pick, [shaped((rows, wide), BF16)] * half_chips, [who, grad_gated], [SMEM, VMEM]
    )
    other_weight = swap(conv_weight, "fsdp", 1)
    weight = call(
        stack_weight, [shaped((3 * wide, C), BF16)], [conv_weight, other_weight], [VMEM] * 2
    )[0]
    table = exchange(jnp.broadcast_to(source_seg[None], (peers, 1, seg_count)), "fsdp").reshape(peers, seg_count)
    grads = [picked[0], swap(picked[1], "fsdp", 2), swap(picked[1], "fsdp", 6)]
    own_stack = call(
        stack, [shaped((own_class, C), BF16)], own_rows, [VMEM] * chips, after=[table, picked[0]]
    )[0]
    other_stack = swap(own_stack, "fsdp", 1)
    act, sent = call(
        forward,
        [shaped((own_class, wide), F32), shaped((own_class + rows, wide), BF16)],
        [who, table, weight, own_stack, other_stack, picked[0]],
        [SMEM, SMEM] + [VMEM] * 4,
        [pltpu.VMEM((all_rows, C), BF16), pltpu.VMEM((all_rows + SEG, 2 * wide), F32)],
        after=grads[1:],
    )
    partner = swap(sent, "fsdp", peers // 2)
    far_own = [swap(own_stack, "dp", d) for d in (1, 2, 3)]
    follow = call(
        functools.partial(follows, chips),
        [shaped((peers * seg_count,), jnp.int32)],
        [who, table],
        [SMEM, SMEM],
        out_specs=[SMEM],
        after=[sent],
    )[0]

    *gated, pre = call(
        gate,
        [shaped((rows, wide), BF16)] * half_chips + [shaped((own_class, wide), BF16)],
        [who, act, partner, *grads],
        [SMEM] + [VMEM] * (2 + len(grads)),
    )
    other_pre = swap(pre, "fsdp", 1)
    *sends, here = call(
        input_grad,
        [shaped((rows + rows // fold, C), BF16)]
        + [shaped((rows, C), BF16)] * (chips - 2)
        + [shaped((rows, 3 * wide), BF16)],
        [follow, pre, other_pre, weight, gated[1]],
        [SMEM, VMEM, VMEM, VMEM, VMEM],
        [pltpu.VMEM((all_rows + SEG, wide), F32), pltpu.VMEM((own_class, 3 * wide), F32)],
    )
    parts = [swap(part, "fsdp", 2 * (k + 1)) for k, part in enumerate(sends)]
    sent_pre = call(
        spread,
        [shaped((groups, all_rows + 16, width), BF16)],
        [follow, pre, other_pre],
        [SMEM, VMEM, VMEM],
    )[0]
    all_pre = exchange(sent_pre, "dp")
    kept = call(
        local, [shaped((rows, C), F32)], [here, weight], [VMEM] * 2, after=[sent_pre]
    )[0]
    grad_in, gated_out = call(
        finish,
        [shaped((rows, C), BF16), shaped((rows, H), BF16)],
        [who, kept, gated[0], *parts],
        [SMEM] + [VMEM] * (chips + 1),
    )
    far_own = held(far_own, [all_pre])
    far_other = [swap(block, "fsdp", 1) for block in far_own]
    blocks = [own_stack, other_stack] + [block for pair in zip(far_own, far_other) for block in pair]
    grad_weight = call(
        functools.partial(weight_grad, 1.0 / math.sqrt(all_rows * groups)),
        [shaped((width, 3 * C), F32)],
        [group[None], all_pre, *blocks],
        [SMEM] + [VMEM] * (1 + len(blocks)),
        [
            pltpu.VMEM((groups, all_rows + SEG, width), F32),
            pltpu.VMEM((groups * all_rows, 3 * width), F32),
            pltpu.VMEM((groups * all_rows, C), BF16),
            pltpu.VMEM((groups, 16, width), jnp.int32),
            pltpu.SMEM((groups, 16, width), jnp.int32),
            pltpu.SemaphoreType.DMA,
        ],
        room=24,
    )[0]
    return gated_out, grad_in, grad_weight


def tap_starts(context_row_block):
    return [context_row_block - (2 - selected_index) * DILATION_SIZE for selected_index in range(3)]


def by_rows(signal, grad_gated, conv_weight, source_seg):
    peer_count = lax.axis_size("fsdp")
    seg_count = source_seg.shape[1]
    row_count = signal.shape[0]
    seg_rows = row_count // seg_count
    context_row_block = 2 * DILATION_SIZE
    starts = tap_starts(context_row_block)
    segments = signal.reshape(seg_count, seg_rows, C)
    sources = source_seg[0]
    source_dev = jnp.where(sources >= 0, sources // seg_count, -1)
    peers = jnp.arange(peer_count, dtype=jnp.int32)
    request_mask = (source_dev[None, :] == peers[:, None]).astype(jnp.int32)
    asked = lax.all_to_all(request_mask, "fsdp", split_axis=0, concat_axis=0, tiled=True)
    send_table = asked.astype(jnp.bfloat16)
    recv_table = (source_dev[:, None] == peers[None, :]).astype(jnp.bfloat16)
    outgoing = jnp.einsum(
        "ns,slc->nlc", send_table, segments, preferred_element_type=jnp.float32
    ).astype(jnp.bfloat16)
    incoming = lax.all_to_all(outgoing, "fsdp", split_axis=0, concat_axis=0, tiled=True)
    carries = jnp.einsum(
        "sn,nlc->slc", recv_table, incoming, preferred_element_type=jnp.float32
    ).astype(jnp.bfloat16)
    extended = jnp.concatenate([carries, segments], axis=1)
    full_weight = lax.all_gather(conv_weight, "fsdp", axis=0, tiled=True)
    contract_final_axis = (((1,), (1,)), ((), ()))
    contract_first = (((0,), (0,)), ((), ()))
    windows = [extended[:, start : start + seg_rows, :].reshape(row_count, C) for start in starts]
    preact = sum(
        (
            lax.dot_general(
                windows[selected_index],
                full_weight[:, selected_index * C : (selected_index + 1) * C],
                contract_final_axis,
                preferred_element_type=jnp.float32,
            )
            for selected_index in range(3)
        )
    )
    filter_act = jnp.tanh(preact[:, :H])
    gate_act = jax.nn.sigmoid(preact[:, H:])
    gated_out = (filter_act * gate_act).astype(jnp.bfloat16)
    upstream_wide = grad_gated.astype(jnp.float32)
    grad_pre = jnp.concatenate(
        [
            upstream_wide * gate_act * (1.0 - filter_act * filter_act),
            upstream_wide * filter_act * gate_act * (1.0 - gate_act),
        ],
        axis=1,
    ).astype(jnp.bfloat16)
    partial_value = jnp.concatenate(
        [
            lax.dot_general(
                grad_pre,
                windows[selected_index],
                contract_first,
                preferred_element_type=jnp.float32,
            ).astype(jnp.bfloat16)
            for selected_index in range(3)
        ],
        axis=1,
    )
    arrived = lax.all_to_all(partial_value, "fsdp", split_axis=0, concat_axis=0, tiled=True)
    shard_sum = jnp.sum(arrived.reshape(peer_count, -1, 3 * C), axis=0, dtype=jnp.float32)
    group_total = lax.psum(shard_sum, "dp")
    total_token_count = row_count * peer_count * lax.axis_size("dp")
    grad_weight = group_total * (1.0 / math.sqrt(total_token_count))
    back_proj = jnp.dot(grad_pre, full_weight, preferred_element_type=jnp.float32)
    back_proj = back_proj.reshape(seg_count, seg_rows, 3 * C)
    grad_ext = jnp.zeros((seg_count, context_row_block + seg_rows, C), jnp.float32)
    for selected_index, start in enumerate(starts):
        grad_ext = grad_ext.at[:, start : start + seg_rows, :].add(
            back_proj[:, :, selected_index * C : (selected_index + 1) * C]
        )
    outgoing_grad = jnp.einsum(
        "sn,slc->nlc",
        recv_table.astype(jnp.float32),
        grad_ext[:, :context_row_block, :],
        precision=lax.Precision.HIGHEST,
    )
    incoming_grad = lax.all_to_all(outgoing_grad, "fsdp", split_axis=0, concat_axis=0, tiled=True)
    tail_grad = jnp.einsum(
        "ns,nlc->slc",
        send_table.astype(jnp.float32),
        incoming_grad,
        precision=lax.Precision.HIGHEST,
    )
    grad_in = (
        grad_ext[:, context_row_block:, :].at[:, seg_rows - context_row_block :, :].add(tail_grad)
    )
    grad_in = grad_in.reshape(row_count, C).astype(jnp.bfloat16)
    return (gated_out, grad_in, grad_weight)


def per_device(signal, grad_gated, conv_weight, source_seg):
    peers, groups = lax.axis_size("fsdp"), lax.axis_size("dp")
    rows, seg_count = signal.shape[0], source_seg.shape[1]
    fits = (
        rows == SEG * seg_count
        and conv_weight.shape[0] % 128 == 0
        and peers & (peers - 1) == 0
        and groups & (groups - 1) == 0
        and peers == 8
        and groups == 4
        and groups * peers * rows <= 2048
        and rows % 64 == 0
        and peers * seg_count <= 128
    )
    plan = by_channels if fits else by_rows
    return plan(signal, grad_gated, conv_weight, source_seg)


def solution(mesh):
    placed = (
        P(("dp", "fsdp"), None),
        P(("dp", "fsdp"), None),
        P("fsdp", None),
        P(("dp", "fsdp"), None),
    )
    return jax.shard_map(
        per_device,
        mesh=mesh,
        in_specs=placed,
        out_specs=(P(("dp", "fsdp"), None), P(("dp", "fsdp"), None), P("fsdp", None)),
        check_vma=False,
    )
```

```python
import functools
import math

import jax
import jax.numpy as jnp
from jax import lax
from jax.experimental import pallas as pl
from jax.experimental.pallas import tpu as pltpu
from jax.sharding import PartitionSpec as P

C = 1024
H = 512
DILATION_SIZE = 4
SEG = 8
BF16 = jnp.bfloat16
F32 = jnp.float32
VMEM = pl.BlockSpec(memory_space=pltpu.VMEM)
SMEM = pl.BlockSpec(memory_space=pltpu.SMEM)
ANY = pl.BlockSpec(memory_space=pl.ANY)
HBM = pl.BlockSpec(memory_space=pltpu.HBM)


def swap(value, axis, distance):
    count = lax.axis_size(axis)
    return lax.ppermute(value, axis, [(i, i ^ distance) for i in range(count)])


def exchange(copies, axis):
    return lax.all_to_all(copies, axis, split_axis=0, concat_axis=0, tiled=True)


def call(body, out_shapes, inputs, specs, scratch=(), out_specs=None, after=(), work=1e10, room=12):
    def run(*refs):
        body(*refs[len(after) :])

    return pl.pallas_call(
        run,
        out_shape=out_shapes,
        in_specs=[ANY] * len(after) + list(specs),
        out_specs=out_specs if out_specs is not None else [VMEM] * len(out_shapes),
        scratch_shapes=list(scratch),
        compiler_params=pltpu.CompilerParams(vmem_limit_bytes=room * 1024 * 1024),
        cost_estimate=pl.CostEstimate(flops=int(work), bytes_accessed=0, transcendentals=0),
    )(*after, *inputs)


def shaped(shape, dtype):
    return jax.ShapeDtypeStruct(shape, dtype)


def roll_half(first, second):
    row = lax.broadcasted_iota(jnp.int32, first.shape, 0)
    return pltpu.roll(jnp.where(row >= 4, first, second), 4, 0)


def pick(grad_ref, *outs):
    half = outs[0].shape[1] // 2
    q = lax.rem(lax.axis_index("fsdp"), grad_ref.shape[1] // half)
    for pair, out in enumerate(outs):
        for part in range(2):
            start = pl.multiple_of((q ^ (2 * pair + part)) * half, half)
            out[:, part * half : (part + 1) * half] = grad_ref[:, pl.ds(start, half)]


def stack_weight(own_ref, other_ref, out_ref):
    width = own_ref.shape[0]
    for tap in range(3):
        for part, ref in enumerate((own_ref, other_ref)):
            start = (2 * tap + part) * width
            out_ref[start : start + width, :] = ref[:, tap * C : (tap + 1) * C]


def place(source, seg_count, chips, me):
    bits = seg_count.bit_length() - 1
    apart = lax.shift_right_logical(source, jnp.int32(bits)) ^ me
    slot = (apart & 1) * chips + lax.shift_right_logical(apart, jnp.int32(1))
    return slot * seg_count + (source & (seg_count - 1))


def follows(chips, table_ref, follow_ref, row_ref):
    peers, seg_count = table_ref.shape
    me = lax.axis_index("fsdp")
    count = peers * seg_count
    for i in range(count):
        follow_ref[i] = count
    for peer in range(peers):
        slot = place(jnp.int32(peer * seg_count), seg_count, chips, me)
        for position in range(seg_count):
            source = table_ref[peer, position]
            found = place(jnp.maximum(source, 0), seg_count, chips, me)
            follow_ref[jnp.where(source >= 0, found, count)] = slot + position
    lane = lax.broadcasted_iota(jnp.int32, row_ref.shape, 1)
    value = jnp.zeros(row_ref.shape, jnp.int32)
    for segment in range(count):
        value = jnp.where(lane == segment, follow_ref[segment], value)
    row_ref[...] = value.astype(F32).astype(BF16)


def stack(*refs):
    blocks, out_ref = refs[:-1], refs[-1]
    count = blocks[0].shape[0]
    for slot, block in enumerate(blocks):
        out_ref[slot * count : (slot + 1) * count, :] = block[...]


def forward(table_ref, weight_ref, own_ref, other_ref, grad_ref, act_ref, sent_ref, rows_ref, early_ref):
    own_class = own_ref.shape[0]
    peers, seg_count = table_ref.shape
    me = lax.axis_index("fsdp")
    rows_ref[:own_class, :] = own_ref[...]
    rows_ref[own_class:, :] = other_ref[...]
    total = 2 * own_class
    wide = weight_ref.shape[0] // 3
    nt = (((1,), (1,)), ((), ()))
    early_ref[:total, :] = lax.dot_general(
        rows_ref[...], weight_ref[: 2 * wide, :], nt, preferred_element_type=F32
    )
    early_ref[total:, :] = jnp.zeros((SEG, 2 * wide), F32)
    act_ref[...] = lax.dot_general(
        rows_ref[:own_class, :], weight_ref[2 * wide :, :], nt, preferred_element_type=F32
    )
    is_filter = lax.axis_index("fsdp") < lax.axis_size("fsdp") // 2
    for segment in range(own_class // SEG):
        at = segment * SEG
        source = table_ref[me ^ (2 * (segment // seg_count)), segment % seg_count]
        found = place(jnp.maximum(source, 0), seg_count, peers // 2, me)
        source = pl.multiple_of(jnp.where(source >= 0, found * SEG, total), SEG)
        carried = early_ref[pl.ds(source, SEG), :]
        preact = (
            act_ref[at : at + SEG, :]
            + carried[:, :wide]
            + roll_half(carried[:, wide:], early_ref[at : at + SEG, wide:])
        )
        act_ref[at : at + SEG, :] = jnp.where(is_filter, jnp.tanh(preact), jax.nn.sigmoid(preact))
    sent_ref[:own_class, :] = act_ref[...].astype(BF16)
    sent_ref[own_class:, :] = grad_ref[...]


def gate(act_ref, other_ref, *refs):
    grads, outs, pre_ref = list(refs[:-3]), refs[-3:-1], refs[-1]
    count = outs[0].shape[0]
    is_filter = lax.axis_index("fsdp") < lax.axis_size("fsdp") // 2
    slots = len(grads) + 1
    grads.insert(slots // 2, other_ref.at[slots * count :, :])
    for slot, grad in enumerate(grads):
        at = slot * count
        there = (slot ^ (slots // 2)) * count
        mine = act_ref[at : at + count, :]
        theirs = other_ref[there : there + count, :].astype(F32)
        upstream = grad[...].astype(F32)
        if slot < len(outs):
            outs[slot][...] = (mine * theirs).astype(BF16)
        for_filter = upstream * theirs * (1.0 - mine * mine)
        for_gate = upstream * theirs * mine * (1.0 - mine)
        pre_ref[at : at + count, :] = jnp.where(is_filter, for_filter, for_gate).astype(BF16)


def input_grad(follow_ref, own_ref, other_ref, weight_ref, gated_ref, *refs):
    sends, here_ref, pre_ref, routed_ref = refs[:-3], refs[-3], refs[-2], refs[-1]
    total, wide = own_ref.shape
    width = wide // 2
    pre_ref[:total, :] = own_ref[...].astype(F32)
    pre_ref[total : 2 * total, :width] = other_ref[:, width:].astype(F32)
    pre_ref[total : 2 * total, width:] = other_ref[:, :width].astype(F32)
    pre_ref[2 * total :, :] = jnp.zeros((SEG, wide), F32)
    for segment in range(total // SEG):
        at = segment * SEG
        follow = pl.multiple_of(follow_ref[segment] * SEG, SEG)
        carried = pre_ref[pl.ds(follow, SEG), :]
        local = pre_ref[at : at + SEG, :]
        routed_ref[at : at + SEG, :wide] = carried
        routed_ref[at : at + SEG, wide : 2 * wide] = roll_half(local, carried)
        routed_ref[at : at + SEG, 2 * wide :] = local
    count = here_ref.shape[0]
    fold = C // wide
    for i in range(fold):
        piece = gated_ref[i * (count // fold) : (i + 1) * (count // fold), :]
        sends[0][count:, i * wide : (i + 1) * wide] = piece
    routed = routed_ref[...].astype(BF16)
    here_ref[...] = routed[:count, :]
    part = jnp.dot(routed[count:, :], weight_ref[...], preferred_element_type=F32)
    for slot, out in enumerate(sends):
        out[:count, :] = part[slot * count : (slot + 1) * count, :].astype(BF16)


def spread(own_ref, other_ref, row_ref, copies_ref):
    total, wide = own_ref.shape
    width = wide // 2
    for copy in range(copies_ref.shape[0]):
        copies_ref[copy, :total, :] = own_ref[:, :width]
        copies_ref[copy, total : 2 * total, :] = other_ref[:, width:]
        copies_ref[copy, 2 * total :, :] = row_ref[...]


def local(here_ref, weight_ref, out_ref):
    out_ref[...] = jnp.dot(here_ref[...], weight_ref[...], preferred_element_type=F32)


def mark(out_ref):
    out_ref[...] = jnp.zeros(out_ref.shape, out_ref.dtype)


def nothing(*refs):
    pass


def held(values, after):
    return pl.pallas_call(
        nothing,
        out_shape=[shaped(value.shape, value.dtype) for value in values],
        in_specs=[ANY] * (len(values) + len(after)),
        out_specs=[ANY] * len(values),
        input_output_aliases={i: i for i in range(len(values))},
        compiler_params=pltpu.CompilerParams(vmem_limit_bytes=2**20),
        cost_estimate=pl.CostEstimate(flops=10000000, bytes_accessed=0, transcendentals=0),
    )(*values, *after)


def weight_grad(scale, pre_ref, *refs):
    blocks = refs[:-8]
    out_ref, early_ref, routed_ref, rows_ref, wide_ref, follow_ref, sem, sems = refs[-8:]
    groups, total, width = early_ref.shape
    total -= SEG
    for i in range(groups):
        wide_ref[i] = pre_ref[lax.axis_index("dp") ^ i, total:, :].astype(F32).astype(jnp.int32)
    load = pltpu.make_async_copy(wide_ref, follow_ref, sem)
    load.start()
    loads = []
    for i, block in enumerate(blocks):
        rows = pl.ds(i * block.shape[0], block.shape[0])
        loads.append(pltpu.make_async_copy(block, rows_ref.at[rows, :], sems.at[i]))
        loads[-1].start()
    for i in range(groups):
        early_ref[i, :total, :] = pre_ref[lax.axis_index("dp") ^ i, :total, :].astype(F32)
        early_ref[i, total:, :] = jnp.zeros((SEG, width), F32)
    load.wait()
    for i in range(groups):
        for segment in range(total // SEG):
            at = segment * SEG
            follow = pl.multiple_of(follow_ref[i, 0, segment] * SEG, SEG)
            carried = early_ref[i, pl.ds(follow, SEG), :]
            local = early_ref[i, at : at + SEG, :]
            at += i * total
            routed_ref[at : at + SEG, :width] = carried
            routed_ref[at : at + SEG, width : 2 * width] = roll_half(local, carried)
            routed_ref[at : at + SEG, 2 * width :] = local
    routed = routed_ref[...].astype(BF16)
    for one in loads:
        one.wait()
    product = lax.dot_general(routed, rows_ref[...], (((0,), (0,)), ((), ())), preferred_element_type=F32)
    for tap in range(3):
        out_ref[:, tap * C : (tap + 1) * C] = product[tap * width : (tap + 1) * width, :] * scale


def finish(kept_ref, gated_ref, *refs):
    parts, (grad_ref, out_ref) = refs[:-2], refs[-2:]
    count = grad_ref.shape[0]
    total = kept_ref[...]
    for part in parts:
        total = total + part[:count, :].astype(F32)
    grad_ref[...] = total.astype(BF16)
    wide = gated_ref.shape[1]
    width = wide // 2
    fold = C // wide
    short = count // fold
    q = lax.rem(lax.axis_index("fsdp"), out_ref.shape[1] // width)
    for part in range(2):
        here = slice(part * width, (part + 1) * width)
        out_ref[:, pl.ds(pl.multiple_of((q ^ part) * width, width), width)] = gated_ref[:, here]
        start = pl.multiple_of((q ^ (2 + part)) * width, width)
        for i in range(fold):
            piece = parts[0][count:, i * wide + part * width : i * wide + (part + 1) * width]
            out_ref[i * short : (i + 1) * short, pl.ds(start, width)] = piece


def by_channels(signal, grad_gated, conv_weight, source_seg):
    peers, groups = lax.axis_size("fsdp"), lax.axis_size("dp")
    chips = peers // 2
    seg_count = source_seg.shape[1]
    rows, width = signal.shape[0], conv_weight.shape[0]
    own_class, all_rows = chips * rows, peers * rows
    wide = 2 * width
    half_chips = chips // 2

    fold = C // wide
    own_rows = [signal] + [swap(signal, "fsdp", 2 * k) for k in range(1, chips)]
    picked = call(
        pick, [shaped((rows, wide), BF16)] * half_chips, [grad_gated], [VMEM]
    )
    other_weight = swap(conv_weight, "fsdp", 1)
    weight = call(
        stack_weight, [shaped((3 * wide, C), BF16)], [conv_weight, other_weight], [VMEM] * 2
    )[0]
    table = exchange(jnp.broadcast_to(source_seg[None], (peers, 1, seg_count)), "fsdp").reshape(peers, seg_count)
    grads = [picked[0], swap(picked[1], "fsdp", 2), swap(picked[1], "fsdp", 6)]
    own_stack = call(
        stack, [shaped((own_class, C), BF16)], own_rows, [VMEM] * chips, after=[table, picked[0]]
    )[0]
    other_stack = swap(own_stack, "fsdp", 1)
    act, sent = call(
        forward,
        [shaped((own_class, wide), F32), shaped((own_class + rows, wide), BF16)],
        [table, weight, own_stack, other_stack, picked[0]],
        [SMEM] + [VMEM] * 4,
        [pltpu.VMEM((all_rows, C), BF16), pltpu.VMEM((all_rows + SEG, 2 * wide), F32)],
        after=grads[1:],
    )
    partner = swap(sent, "fsdp", peers // 2)
    far_own = [swap(own_stack, "dp", d) for d in (1, 2, 3)]
    follow, follow_row = call(
        functools.partial(follows, chips),
        [shaped((peers * seg_count + 1,), jnp.int32), shaped((16, width), BF16)],
        [table],
        [SMEM],
        out_specs=[SMEM, VMEM],
        after=[sent],
    )

    *gated, pre = call(
        gate,
        [shaped((rows, wide), BF16)] * half_chips + [shaped((own_class, wide), BF16)],
        [act, partner, *grads],
        [VMEM] * (2 + len(grads)),
    )
    other_pre = swap(pre, "fsdp", 1)
    *sends, here = call(
        input_grad,
        [shaped((rows + rows // fold, C), BF16)]
        + [shaped((rows, C), BF16)] * (chips - 2)
        + [shaped((rows, 3 * wide), BF16)],
        [follow, pre, other_pre, weight, gated[1]],
        [SMEM, VMEM, VMEM, VMEM, VMEM],
        [pltpu.VMEM((all_rows + SEG, wide), F32), pltpu.VMEM((own_class, 3 * wide), F32)],
    )
    parts = [swap(part, "fsdp", 2 * (k + 1)) for k, part in enumerate(sends)]
    sent_pre = call(
        spread,
        [shaped((groups, all_rows + 16, width), BF16)],
        [pre, other_pre, follow_row],
        [VMEM] * 3,
    )[0]
    all_pre = exchange(sent_pre, "dp")
    kept = call(
        local, [shaped((rows, C), F32)], [here, weight], [VMEM] * 2, after=[sent_pre, *far_own]
    )[0]
    grad_in, gated_out = call(
        finish,
        [shaped((rows, C), BF16), shaped((rows, H), BF16)],
        [kept, gated[0], *parts],
        [VMEM] * (chips + 1),
    )
    far_own = held(far_own, [kept])
    far_other = [swap(block, "fsdp", 1) for block in far_own]
    blocks = [own_stack, other_stack] + [block for pair in zip(far_own, far_other) for block in pair]
    grad_weight = call(
        functools.partial(weight_grad, 1.0 / math.sqrt(all_rows * groups)),
        [shaped((width, 3 * C), F32)],
        [all_pre, *blocks],
        [VMEM] + [ANY] * len(blocks),
        [
            pltpu.VMEM((groups, all_rows + SEG, width), F32),
            pltpu.VMEM((groups * all_rows, 3 * width), F32),
            pltpu.VMEM((groups * all_rows, C), BF16),
            pltpu.VMEM((groups, 16, width), jnp.int32),
            pltpu.SMEM((groups, 16, width), jnp.int32),
            pltpu.SemaphoreType.DMA,
            pltpu.SemaphoreType.DMA((len(blocks),)),
        ],
        room=24,
    )[0]
    return gated_out, grad_in, grad_weight


def tap_starts(context_row_block):
    return [context_row_block - (2 - selected_index) * DILATION_SIZE for selected_index in range(3)]


def by_rows(signal, grad_gated, conv_weight, source_seg):
    peer_count = lax.axis_size("fsdp")
    seg_count = source_seg.shape[1]
    row_count = signal.shape[0]
    seg_rows = row_count // seg_count
    context_row_block = 2 * DILATION_SIZE
    starts = tap_starts(context_row_block)
    segments = signal.reshape(seg_count, seg_rows, C)
    sources = source_seg[0]
    source_dev = jnp.where(sources >= 0, sources // seg_count, -1)
    peers = jnp.arange(peer_count, dtype=jnp.int32)
    request_mask = (source_dev[None, :] == peers[:, None]).astype(jnp.int32)
    asked = lax.all_to_all(request_mask, "fsdp", split_axis=0, concat_axis=0, tiled=True)
    send_table = asked.astype(jnp.bfloat16)
    recv_table = (source_dev[:, None] == peers[None, :]).astype(jnp.bfloat16)
    outgoing = jnp.einsum(
        "ns,slc->nlc", send_table, segments, preferred_element_type=jnp.float32
    ).astype(jnp.bfloat16)
    incoming = lax.all_to_all(outgoing, "fsdp", split_axis=0, concat_axis=0, tiled=True)
    carries = jnp.einsum(
        "sn,nlc->slc", recv_table, incoming, preferred_element_type=jnp.float32
    ).astype(jnp.bfloat16)
    extended = jnp.concatenate([carries, segments], axis=1)
    full_weight = lax.all_gather(conv_weight, "fsdp", axis=0, tiled=True)
    contract_final_axis = (((1,), (1,)), ((), ()))
    contract_first = (((0,), (0,)), ((), ()))
    windows = [extended[:, start : start + seg_rows, :].reshape(row_count, C) for start in starts]
    preact = sum(
        (
            lax.dot_general(
                windows[selected_index],
                full_weight[:, selected_index * C : (selected_index + 1) * C],
                contract_final_axis,
                preferred_element_type=jnp.float32,
            )
            for selected_index in range(3)
        )
    )
    filter_act = jnp.tanh(preact[:, :H])
    gate_act = jax.nn.sigmoid(preact[:, H:])
    gated_out = (filter_act * gate_act).astype(jnp.bfloat16)
    upstream_wide = grad_gated.astype(jnp.float32)
    grad_pre = jnp.concatenate(
        [
            upstream_wide * gate_act * (1.0 - filter_act * filter_act),
            upstream_wide * filter_act * gate_act * (1.0 - gate_act),
        ],
        axis=1,
    ).astype(jnp.bfloat16)
    partial_value = jnp.concatenate(
        [
            lax.dot_general(
                grad_pre,
                windows[selected_index],
                contract_first,
                preferred_element_type=jnp.float32,
            ).astype(jnp.bfloat16)
            for selected_index in range(3)
        ],
        axis=1,
    )
    arrived = lax.all_to_all(partial_value, "fsdp", split_axis=0, concat_axis=0, tiled=True)
    shard_sum = jnp.sum(arrived.reshape(peer_count, -1, 3 * C), axis=0, dtype=jnp.float32)
    group_total = lax.psum(shard_sum, "dp")
    total_token_count = row_count * peer_count * lax.axis_size("dp")
    grad_weight = group_total * (1.0 / math.sqrt(total_token_count))
    back_proj = jnp.dot(grad_pre, full_weight, preferred_element_type=jnp.float32)
    back_proj = back_proj.reshape(seg_count, seg_rows, 3 * C)
    grad_ext = jnp.zeros((seg_count, context_row_block + seg_rows, C), jnp.float32)
    for selected_index, start in enumerate(starts):
        grad_ext = grad_ext.at[:, start : start + seg_rows, :].add(
            back_proj[:, :, selected_index * C : (selected_index + 1) * C]
        )
    outgoing_grad = jnp.einsum(
        "sn,slc->nlc",
        recv_table.astype(jnp.float32),
        grad_ext[:, :context_row_block, :],
        precision=lax.Precision.HIGHEST,
    )
    incoming_grad = lax.all_to_all(outgoing_grad, "fsdp", split_axis=0, concat_axis=0, tiled=True)
    tail_grad = jnp.einsum(
        "ns,nlc->slc",
        send_table.astype(jnp.float32),
        incoming_grad,
        precision=lax.Precision.HIGHEST,
    )
    grad_in = (
        grad_ext[:, context_row_block:, :].at[:, seg_rows - context_row_block :, :].add(tail_grad)
    )
    grad_in = grad_in.reshape(row_count, C).astype(jnp.bfloat16)
    return (gated_out, grad_in, grad_weight)


def per_device(signal, grad_gated, conv_weight, source_seg):
    peers, groups = lax.axis_size("fsdp"), lax.axis_size("dp")
    rows, seg_count = signal.shape[0], source_seg.shape[1]
    fits = (
        rows == SEG * seg_count
        and conv_weight.shape[0] % 128 == 0
        and peers & (peers - 1) == 0
        and groups & (groups - 1) == 0
        and peers == 8
        and groups == 4
        and groups * peers * rows <= 2048
        and rows % 64 == 0
        and peers * seg_count <= 128
        and seg_count & (seg_count - 1) == 0
    )
    plan = by_channels if fits else by_rows
    return plan(signal, grad_gated, conv_weight, source_seg)


def solution(mesh):
    placed = (
        P(("dp", "fsdp"), None),
        P(("dp", "fsdp"), None),
        P("fsdp", None),
        P(("dp", "fsdp"), None),
    )
    return jax.shard_map(
        per_device,
        mesh=mesh,
        in_specs=placed,
        out_specs=(P(("dp", "fsdp"), None), P(("dp", "fsdp"), None), P("fsdp", None)),
        check_vma=False,
    )
```

```python
import functools
import math

import jax
import jax.numpy as jnp
from jax import lax
from jax.experimental import pallas as pl
from jax.experimental.pallas import tpu as pltpu
from jax.sharding import PartitionSpec as P

C = 1024
H = 512
DILATION_SIZE = 4
SEG = 8
LOADED = (0, 3, 5, 7)
BF16 = jnp.bfloat16
F32 = jnp.float32
VMEM = pl.BlockSpec(memory_space=pltpu.VMEM)
SMEM = pl.BlockSpec(memory_space=pltpu.SMEM)
ANY = pl.BlockSpec(memory_space=pl.ANY)
HBM = pl.BlockSpec(memory_space=pltpu.HBM)


def swap(value, axis, distance):
    count = lax.axis_size(axis)
    return lax.ppermute(value, axis, [(i, i ^ distance) for i in range(count)])


def exchange(copies, axis):
    return lax.all_to_all(copies, axis, split_axis=0, concat_axis=0, tiled=True)


def call(body, out_shapes, inputs, specs, scratch=(), out_specs=None, after=(), work=1e10, room=12):
    def run(*refs):
        body(*refs[len(after) :])

    return pl.pallas_call(
        run,
        out_shape=out_shapes,
        in_specs=[ANY] * len(after) + list(specs),
        out_specs=out_specs if out_specs is not None else [VMEM] * len(out_shapes),
        scratch_shapes=list(scratch),
        compiler_params=pltpu.CompilerParams(vmem_limit_bytes=room * 1024 * 1024),
        cost_estimate=pl.CostEstimate(flops=int(work), bytes_accessed=0, transcendentals=0),
    )(*after, *inputs)


def shaped(shape, dtype):
    return jax.ShapeDtypeStruct(shape, dtype)


def roll_half(first, second):
    row = lax.broadcasted_iota(jnp.int32, first.shape, 0)
    return pltpu.roll(jnp.where(row >= 4, first, second), 4, 0)


def pick(grad_ref, *outs):
    half = outs[0].shape[1] // 2
    q = lax.rem(lax.axis_index("fsdp"), grad_ref.shape[1] // half)
    for pair, out in enumerate(outs):
        for part in range(2):
            start = pl.multiple_of((q ^ (2 * pair + part)) * half, half)
            out[:, part * half : (part + 1) * half] = grad_ref[:, pl.ds(start, half)]


def stack_weight(own_ref, other_ref, out_ref):
    width = own_ref.shape[0]
    for tap in range(3):
        for part, ref in enumerate((own_ref, other_ref)):
            start = (2 * tap + part) * width
            out_ref[start : start + width, :] = ref[:, tap * C : (tap + 1) * C]


def place(source, seg_count, chips, me):
    bits = seg_count.bit_length() - 1
    apart = lax.shift_right_logical(source, jnp.int32(bits)) ^ me
    slot = (apart & 1) * chips + lax.shift_right_logical(apart, jnp.int32(1))
    return slot * seg_count + (source & (seg_count - 1))


def follows(chips, table_ref, follow_ref, row_ref):
    peers, seg_count = table_ref.shape
    me = lax.axis_index("fsdp")
    count = peers * seg_count
    for i in range(count):
        follow_ref[i] = count
    for peer in range(peers):
        slot = place(jnp.int32(peer * seg_count), seg_count, chips, me)
        for position in range(seg_count):
            source = table_ref[peer, position]
            found = place(jnp.maximum(source, 0), seg_count, chips, me)
            follow_ref[jnp.where(source >= 0, found, count)] = slot + position
    lane = lax.broadcasted_iota(jnp.int32, row_ref.shape, 1)
    value = jnp.zeros(row_ref.shape, jnp.int32)
    for segment in range(count):
        value = jnp.where(lane == segment, follow_ref[segment], value)
    row_ref[...] = value.astype(F32).astype(BF16)


def stack(*refs):
    blocks, out_ref = refs[:-1], refs[-1]
    count = blocks[0].shape[0]
    for slot, block in enumerate(blocks):
        out_ref[slot * count : (slot + 1) * count, :] = block[...]


def forward(table_ref, weight_ref, own_ref, other_ref, grad_ref, act_ref, sent_ref, rows_ref, early_ref):
    own_class = own_ref.shape[0]
    peers, seg_count = table_ref.shape
    me = lax.axis_index("fsdp")
    rows_ref[:own_class, :] = own_ref[...]
    rows_ref[own_class:, :] = other_ref[...]
    total = 2 * own_class
    wide = weight_ref.shape[0] // 3
    nt = (((1,), (1,)), ((), ()))
    early_ref[:total, :] = lax.dot_general(
        rows_ref[...], weight_ref[: 2 * wide, :], nt, preferred_element_type=F32
    )
    early_ref[total:, :] = jnp.zeros((SEG, 2 * wide), F32)
    act_ref[...] = lax.dot_general(
        rows_ref[:own_class, :], weight_ref[2 * wide :, :], nt, preferred_element_type=F32
    )
    is_filter = lax.axis_index("fsdp") < lax.axis_size("fsdp") // 2
    for segment in range(own_class // SEG):
        at = segment * SEG
        source = table_ref[me ^ (2 * (segment // seg_count)), segment % seg_count]
        found = place(jnp.maximum(source, 0), seg_count, peers // 2, me)
        source = pl.multiple_of(jnp.where(source >= 0, found * SEG, total), SEG)
        carried = early_ref[pl.ds(source, SEG), :]
        preact = (
            act_ref[at : at + SEG, :]
            + carried[:, :wide]
            + roll_half(carried[:, wide:], early_ref[at : at + SEG, wide:])
        )
        act_ref[at : at + SEG, :] = jnp.where(is_filter, jnp.tanh(preact), jax.nn.sigmoid(preact))
    sent_ref[:own_class, :] = act_ref[...].astype(BF16)
    sent_ref[own_class:, :] = grad_ref[...]


def gate(act_ref, other_ref, *refs):
    grads, outs, pre_ref = list(refs[:-3]), refs[-3:-1], refs[-1]
    count = outs[0].shape[0]
    is_filter = lax.axis_index("fsdp") < lax.axis_size("fsdp") // 2
    slots = len(grads) + 1
    grads.insert(slots // 2, other_ref.at[slots * count :, :])
    for slot, grad in enumerate(grads):
        at = slot * count
        there = (slot ^ (slots // 2)) * count
        mine = act_ref[at : at + count, :]
        theirs = other_ref[there : there + count, :].astype(F32)
        upstream = grad[...].astype(F32)
        if slot < len(outs):
            outs[slot][...] = (mine * theirs).astype(BF16)
        for_filter = upstream * theirs * (1.0 - mine * mine)
        for_gate = upstream * theirs * mine * (1.0 - mine)
        pre_ref[at : at + count, :] = jnp.where(is_filter, for_filter, for_gate).astype(BF16)


def input_grad(follow_ref, own_ref, other_ref, weight_ref, gated_ref, *refs):
    sends, here_ref, pre_ref, routed_ref = refs[:-3], refs[-3], refs[-2], refs[-1]
    total, wide = own_ref.shape
    width = wide // 2
    pre_ref[:total, :] = own_ref[...].astype(F32)
    pre_ref[total : 2 * total, :width] = other_ref[:, width:].astype(F32)
    pre_ref[total : 2 * total, width:] = other_ref[:, :width].astype(F32)
    pre_ref[2 * total :, :] = jnp.zeros((SEG, wide), F32)
    for segment in range(total // SEG):
        at = segment * SEG
        follow = pl.multiple_of(follow_ref[segment] * SEG, SEG)
        carried = pre_ref[pl.ds(follow, SEG), :]
        local = pre_ref[at : at + SEG, :]
        routed_ref[at : at + SEG, :wide] = carried
        routed_ref[at : at + SEG, wide : 2 * wide] = roll_half(local, carried)
        routed_ref[at : at + SEG, 2 * wide :] = local
    count = here_ref.shape[0]
    fold = C // wide
    for i in range(fold):
        piece = gated_ref[i * (count // fold) : (i + 1) * (count // fold), :]
        sends[0][count:, i * wide : (i + 1) * wide] = piece
    routed = routed_ref[...].astype(BF16)
    here_ref[...] = routed[:count, :]
    part = jnp.dot(routed[count:, :], weight_ref[...], preferred_element_type=F32)
    for slot, out in enumerate(sends):
        out[:count, :] = part[slot * count : (slot + 1) * count, :].astype(BF16)


def spread(own_ref, other_ref, row_ref, copies_ref):
    total, wide = own_ref.shape
    width = wide // 2
    for copy in range(copies_ref.shape[0]):
        copies_ref[copy, :total, :] = own_ref[:, :width]
        copies_ref[copy, total : 2 * total, :] = other_ref[:, width:]
        copies_ref[copy, 2 * total :, :] = row_ref[...]


def local(here_ref, weight_ref, out_ref):
    out_ref[...] = jnp.dot(here_ref[...], weight_ref[...], preferred_element_type=F32)


def mark(out_ref):
    out_ref[...] = jnp.zeros(out_ref.shape, out_ref.dtype)


def nothing(*refs):
    pass


def held(values, after):
    return pl.pallas_call(
        nothing,
        out_shape=[shaped(value.shape, value.dtype) for value in values],
        in_specs=[ANY] * (len(values) + len(after)),
        out_specs=[ANY] * len(values),
        input_output_aliases={i: i for i in range(len(values))},
        compiler_params=pltpu.CompilerParams(vmem_limit_bytes=2**20),
        cost_estimate=pl.CostEstimate(flops=10000000, bytes_accessed=0, transcendentals=0),
    )(*values, *after)


def weight_grad(scale, pre_ref, *refs):
    blocks = refs[:-8]
    out_ref, early_ref, routed_ref, rows_ref, wide_ref, follow_ref, sem, sems = refs[-8:]
    groups, total, width = early_ref.shape
    total -= SEG
    for i in range(groups):
        wide_ref[i] = pre_ref[lax.axis_index("dp") ^ i, total:, :].astype(F32).astype(jnp.int32)
    load = pltpu.make_async_copy(wide_ref, follow_ref, sem)
    load.start()
    loads = []
    count = blocks[0].shape[0]
    for i in LOADED:
        rows = pl.ds(i * count, count)
        loads.append(pltpu.make_async_copy(blocks[i], rows_ref.at[rows, :], sems.at[i]))
        loads[-1].start()
    for i, block in enumerate(blocks):
        if i not in LOADED:
            rows_ref[i * count : (i + 1) * count, :] = block[...]
    for i in range(groups):
        early_ref[i, :total, :] = pre_ref[lax.axis_index("dp") ^ i, :total, :].astype(F32)
        early_ref[i, total:, :] = jnp.zeros((SEG, width), F32)
    load.wait()
    for i in range(groups):
        for segment in range(total // SEG):
            at = segment * SEG
            follow = pl.multiple_of(follow_ref[i, 0, segment] * SEG, SEG)
            carried = early_ref[i, pl.ds(follow, SEG), :]
            local = early_ref[i, at : at + SEG, :]
            at += i * total
            routed_ref[at : at + SEG, :width] = carried
            routed_ref[at : at + SEG, width : 2 * width] = roll_half(local, carried)
            routed_ref[at : at + SEG, 2 * width :] = local
    routed = routed_ref[...].astype(BF16)
    for one in loads:
        one.wait()
    product = lax.dot_general(routed, rows_ref[...], (((0,), (0,)), ((), ())), preferred_element_type=F32)
    for tap in range(3):
        out_ref[:, tap * C : (tap + 1) * C] = product[tap * width : (tap + 1) * width, :] * scale


def finish(kept_ref, gated_ref, *refs):
    parts, (grad_ref, out_ref) = refs[:-2], refs[-2:]
    count = grad_ref.shape[0]
    total = kept_ref[...]
    for part in parts:
        total = total + part[:count, :].astype(F32)
    grad_ref[...] = total.astype(BF16)
    wide = gated_ref.shape[1]
    width = wide // 2
    fold = C // wide
    short = count // fold
    q = lax.rem(lax.axis_index("fsdp"), out_ref.shape[1] // width)
    for part in range(2):
        here = slice(part * width, (part + 1) * width)
        out_ref[:, pl.ds(pl.multiple_of((q ^ part) * width, width), width)] = gated_ref[:, here]
        start = pl.multiple_of((q ^ (2 + part)) * width, width)
        for i in range(fold):
            piece = parts[0][count:, i * wide + part * width : i * wide + (part + 1) * width]
            out_ref[i * short : (i + 1) * short, pl.ds(start, width)] = piece


def by_channels(signal, grad_gated, conv_weight, source_seg):
    peers, groups = lax.axis_size("fsdp"), lax.axis_size("dp")
    chips = peers // 2
    seg_count = source_seg.shape[1]
    rows, width = signal.shape[0], conv_weight.shape[0]
    own_class, all_rows = chips * rows, peers * rows
    wide = 2 * width
    half_chips = chips // 2

    fold = C // wide
    own_rows = [signal] + [swap(signal, "fsdp", 2 * k) for k in range(1, chips)]
    picked = call(
        pick, [shaped((rows, wide), BF16)] * half_chips, [grad_gated], [VMEM]
    )
    other_weight = swap(conv_weight, "fsdp", 1)
    weight = call(
        stack_weight, [shaped((3 * wide, C), BF16)], [conv_weight, other_weight], [VMEM] * 2
    )[0]
    table = exchange(jnp.broadcast_to(source_seg[None], (peers, 1, seg_count)), "fsdp").reshape(peers, seg_count)
    grads = [picked[0], swap(picked[1], "fsdp", 2), swap(picked[1], "fsdp", 6)]
    own_stack = call(
        stack, [shaped((own_class, C), BF16)], own_rows, [VMEM] * chips, after=[table, picked[0]]
    )[0]
    other_stack = swap(own_stack, "fsdp", 1)
    act, sent = call(
        forward,
        [shaped((own_class, wide), F32), shaped((own_class + rows, wide), BF16)],
        [table, weight, own_stack, other_stack, picked[0]],
        [SMEM] + [VMEM] * 4,
        [pltpu.VMEM((all_rows, C), BF16), pltpu.VMEM((all_rows + SEG, 2 * wide), F32)],
        after=grads[1:],
    )
    partner = swap(sent, "fsdp", peers // 2)
    far_own = [swap(own_stack, "dp", d) for d in (1, 2, 3)]
    follow, follow_row = call(
        functools.partial(follows, chips),
        [shaped((peers * seg_count + 1,), jnp.int32), shaped((16, width), BF16)],
        [table],
        [SMEM],
        out_specs=[SMEM, VMEM],
        after=[sent],
    )

    *gated, pre = call(
        gate,
        [shaped((rows, wide), BF16)] * half_chips + [shaped((own_class, wide), BF16)],
        [act, partner, *grads],
        [VMEM] * (2 + len(grads)),
    )
    other_pre = swap(pre, "fsdp", 1)
    *sends, here = call(
        input_grad,
        [shaped((rows + rows // fold, C), BF16)]
        + [shaped((rows, C), BF16)] * (chips - 2)
        + [shaped((rows, 3 * wide), BF16)],
        [follow, pre, other_pre, weight, gated[1]],
        [SMEM, VMEM, VMEM, VMEM, VMEM],
        [pltpu.VMEM((all_rows + SEG, wide), F32), pltpu.VMEM((own_class, 3 * wide), F32)],
    )
    parts = [swap(part, "fsdp", 2 * (k + 1)) for k, part in enumerate(sends)]
    sent_pre = call(
        spread,
        [shaped((groups, all_rows + 16, width), BF16)],
        [pre, other_pre, follow_row],
        [VMEM] * 3,
    )[0]
    all_pre = exchange(sent_pre, "dp")
    kept = call(
        local, [shaped((rows, C), F32)], [here, weight], [VMEM] * 2, after=[sent_pre]
    )[0]
    arrived = call(mark, [shaped((8, 128), F32)], [], [], after=[kept, *far_own])[0]
    grad_in, gated_out = call(
        finish,
        [shaped((rows, C), BF16), shaped((rows, H), BF16)],
        [kept, gated[0], *parts],
        [VMEM] * (chips + 1),
        after=[arrived],
    )
    far_own = held(far_own, [arrived])
    far_other = [swap(block, "fsdp", 1) for block in far_own]
    blocks = [own_stack, other_stack] + [block for pair in zip(far_own, far_other) for block in pair]
    grad_weight = call(
        functools.partial(weight_grad, 1.0 / math.sqrt(all_rows * groups)),
        [shaped((width, 3 * C), F32)],
        [all_pre, *blocks],
        [VMEM] + [ANY if i in LOADED else VMEM for i in range(len(blocks))],
        [
            pltpu.VMEM((groups, all_rows + SEG, width), F32),
            pltpu.VMEM((groups * all_rows, 3 * width), F32),
            pltpu.VMEM((groups * all_rows, C), BF16),
            pltpu.VMEM((groups, 16, width), jnp.int32),
            pltpu.SMEM((groups, 16, width), jnp.int32),
            pltpu.SemaphoreType.DMA,
            pltpu.SemaphoreType.DMA((len(blocks),)),
        ],
        room=24,
    )[0]
    return gated_out, grad_in, grad_weight


def tap_starts(context_row_block):
    return [context_row_block - (2 - selected_index) * DILATION_SIZE for selected_index in range(3)]


def by_rows(signal, grad_gated, conv_weight, source_seg):
    peer_count = lax.axis_size("fsdp")
    seg_count = source_seg.shape[1]
    row_count = signal.shape[0]
    seg_rows = row_count // seg_count
    context_row_block = 2 * DILATION_SIZE
    starts = tap_starts(context_row_block)
    segments = signal.reshape(seg_count, seg_rows, C)
    sources = source_seg[0]
    source_dev = jnp.where(sources >= 0, sources // seg_count, -1)
    peers = jnp.arange(peer_count, dtype=jnp.int32)
    request_mask = (source_dev[None, :] == peers[:, None]).astype(jnp.int32)
    asked = lax.all_to_all(request_mask, "fsdp", split_axis=0, concat_axis=0, tiled=True)
    send_table = asked.astype(jnp.bfloat16)
    recv_table = (source_dev[:, None] == peers[None, :]).astype(jnp.bfloat16)
    outgoing = jnp.einsum(
        "ns,slc->nlc", send_table, segments, preferred_element_type=jnp.float32
    ).astype(jnp.bfloat16)
    incoming = lax.all_to_all(outgoing, "fsdp", split_axis=0, concat_axis=0, tiled=True)
    carries = jnp.einsum(
        "sn,nlc->slc", recv_table, incoming, preferred_element_type=jnp.float32
    ).astype(jnp.bfloat16)
    extended = jnp.concatenate([carries, segments], axis=1)
    full_weight = lax.all_gather(conv_weight, "fsdp", axis=0, tiled=True)
    contract_final_axis = (((1,), (1,)), ((), ()))
    contract_first = (((0,), (0,)), ((), ()))
    windows = [extended[:, start : start + seg_rows, :].reshape(row_count, C) for start in starts]
    preact = sum(
        (
            lax.dot_general(
                windows[selected_index],
                full_weight[:, selected_index * C : (selected_index + 1) * C],
                contract_final_axis,
                preferred_element_type=jnp.float32,
            )
            for selected_index in range(3)
        )
    )
    filter_act = jnp.tanh(preact[:, :H])
    gate_act = jax.nn.sigmoid(preact[:, H:])
    gated_out = (filter_act * gate_act).astype(jnp.bfloat16)
    upstream_wide = grad_gated.astype(jnp.float32)
    grad_pre = jnp.concatenate(
        [
            upstream_wide * gate_act * (1.0 - filter_act * filter_act),
            upstream_wide * filter_act * gate_act * (1.0 - gate_act),
        ],
        axis=1,
    ).astype(jnp.bfloat16)
    partial_value = jnp.concatenate(
        [
            lax.dot_general(
                grad_pre,
                windows[selected_index],
                contract_first,
                preferred_element_type=jnp.float32,
            ).astype(jnp.bfloat16)
            for selected_index in range(3)
        ],
        axis=1,
    )
    arrived = lax.all_to_all(partial_value, "fsdp", split_axis=0, concat_axis=0, tiled=True)
    shard_sum = jnp.sum(arrived.reshape(peer_count, -1, 3 * C), axis=0, dtype=jnp.float32)
    group_total = lax.psum(shard_sum, "dp")
    total_token_count = row_count * peer_count * lax.axis_size("dp")
    grad_weight = group_total * (1.0 / math.sqrt(total_token_count))
    back_proj = jnp.dot(grad_pre, full_weight, preferred_element_type=jnp.float32)
    back_proj = back_proj.reshape(seg_count, seg_rows, 3 * C)
    grad_ext = jnp.zeros((seg_count, context_row_block + seg_rows, C), jnp.float32)
    for selected_index, start in enumerate(starts):
        grad_ext = grad_ext.at[:, start : start + seg_rows, :].add(
            back_proj[:, :, selected_index * C : (selected_index + 1) * C]
        )
    outgoing_grad = jnp.einsum(
        "sn,slc->nlc",
        recv_table.astype(jnp.float32),
        grad_ext[:, :context_row_block, :],
        precision=lax.Precision.HIGHEST,
    )
    incoming_grad = lax.all_to_all(outgoing_grad, "fsdp", split_axis=0, concat_axis=0, tiled=True)
    tail_grad = jnp.einsum(
        "ns,nlc->slc",
        send_table.astype(jnp.float32),
        incoming_grad,
        precision=lax.Precision.HIGHEST,
    )
    grad_in = (
        grad_ext[:, context_row_block:, :].at[:, seg_rows - context_row_block :, :].add(tail_grad)
    )
    grad_in = grad_in.reshape(row_count, C).astype(jnp.bfloat16)
    return (gated_out, grad_in, grad_weight)


def per_device(signal, grad_gated, conv_weight, source_seg):
    peers, groups = lax.axis_size("fsdp"), lax.axis_size("dp")
    rows, seg_count = signal.shape[0], source_seg.shape[1]
    fits = (
        rows == SEG * seg_count
        and conv_weight.shape[0] % 128 == 0
        and peers & (peers - 1) == 0
        and groups & (groups - 1) == 0
        and peers == 8
        and groups == 4
        and groups * peers * rows <= 2048
        and rows % 64 == 0
        and peers * seg_count <= 128
        and seg_count & (seg_count - 1) == 0
    )
    plan = by_channels if fits else by_rows
    return plan(signal, grad_gated, conv_weight, source_seg)


def solution(mesh):
    placed = (
        P(("dp", "fsdp"), None),
        P(("dp", "fsdp"), None),
        P("fsdp", None),
        P(("dp", "fsdp"), None),
    )
    return jax.shard_map(
        per_device,
        mesh=mesh,
        in_specs=placed,
        out_specs=(P(("dp", "fsdp"), None), P(("dp", "fsdp"), None), P("fsdp", None)),
        check_vma=False,
    )
```

```python
import functools
import math

import jax
import jax.numpy as jnp
from jax import lax
from jax.experimental import pallas as pl
from jax.experimental.pallas import tpu as pltpu
from jax.sharding import PartitionSpec as P

C = 1024
H = 512
DILATION_SIZE = 4
SEG = 8
LOADED = (0, 3, 5, 7)
BF16 = jnp.bfloat16
F32 = jnp.float32
VMEM = pl.BlockSpec(memory_space=pltpu.VMEM)
SMEM = pl.BlockSpec(memory_space=pltpu.SMEM)
ANY = pl.BlockSpec(memory_space=pl.ANY)
HBM = pl.BlockSpec(memory_space=pltpu.HBM)


def swap(value, axis, distance):
    count = lax.axis_size(axis)
    return lax.ppermute(value, axis, [(i, i ^ distance) for i in range(count)])


def exchange(copies, axis):
    return lax.all_to_all(copies, axis, split_axis=0, concat_axis=0, tiled=True)


def call(body, out_shapes, inputs, specs, scratch=(), out_specs=None, after=(), work=1e10, room=12):
    def run(*refs):
        body(*refs[len(after) :])

    return pl.pallas_call(
        run,
        out_shape=out_shapes,
        in_specs=[ANY] * len(after) + list(specs),
        out_specs=out_specs if out_specs is not None else [VMEM] * len(out_shapes),
        scratch_shapes=list(scratch),
        compiler_params=pltpu.CompilerParams(vmem_limit_bytes=room * 1024 * 1024),
        cost_estimate=pl.CostEstimate(flops=int(work), bytes_accessed=0, transcendentals=0),
    )(*after, *inputs)


def shaped(shape, dtype):
    return jax.ShapeDtypeStruct(shape, dtype)


def roll_half(first, second):
    row = lax.broadcasted_iota(jnp.int32, first.shape, 0)
    return pltpu.roll(jnp.where(row >= 4, first, second), 4, 0)


def pick(grad_ref, *outs):
    half = outs[0].shape[1] // 2
    q = lax.rem(lax.axis_index("fsdp"), grad_ref.shape[1] // half)
    for pair, out in enumerate(outs):
        for part in range(2):
            start = pl.multiple_of((q ^ (2 * pair + part)) * half, half)
            out[:, part * half : (part + 1) * half] = grad_ref[:, pl.ds(start, half)]


def stack_weight(own_ref, other_ref, out_ref):
    width = own_ref.shape[0]
    for tap in range(3):
        for part, ref in enumerate((own_ref, other_ref)):
            start = (2 * tap + part) * width
            out_ref[start : start + width, :] = ref[:, tap * C : (tap + 1) * C]


def place(source, seg_count, chips, me):
    bits = seg_count.bit_length() - 1
    apart = lax.shift_right_logical(source, jnp.int32(bits)) ^ me
    slot = (apart & 1) * chips + lax.shift_right_logical(apart, jnp.int32(1))
    return slot * seg_count + (source & (seg_count - 1))


def follows(chips, table_ref, follow_ref, row_ref):
    peers, seg_count = table_ref.shape
    me = lax.axis_index("fsdp")
    count = peers * seg_count
    for i in range(count):
        follow_ref[i] = count
    for peer in range(peers):
        slot = place(jnp.int32(peer * seg_count), seg_count, chips, me)
        for position in range(seg_count):
            source = table_ref[peer, position]
            found = place(jnp.maximum(source, 0), seg_count, chips, me)
            follow_ref[jnp.where(source >= 0, found, count)] = slot + position
    lane = lax.broadcasted_iota(jnp.int32, row_ref.shape, 1)
    value = jnp.zeros(row_ref.shape, jnp.int32)
    for segment in range(count):
        value = jnp.where(lane == segment, follow_ref[segment], value)
    row_ref[...] = value.astype(F32).astype(BF16)


def stack(*refs):
    blocks, out_ref = refs[:-1], refs[-1]
    count = blocks[0].shape[0]
    for slot, block in enumerate(blocks):
        out_ref[slot * count : (slot + 1) * count, :] = block[...]


def forward(table_ref, weight_ref, own_ref, other_ref, grad_ref, act_ref, sent_ref, rows_ref, early_ref):
    own_class = own_ref.shape[0]
    peers, seg_count = table_ref.shape
    me = lax.axis_index("fsdp")
    rows_ref[:own_class, :] = own_ref[...]
    rows_ref[own_class:, :] = other_ref[...]
    total = 2 * own_class
    wide = weight_ref.shape[0] // 3
    nt = (((1,), (1,)), ((), ()))
    early_ref[:total, :] = lax.dot_general(
        rows_ref[...], weight_ref[: 2 * wide, :], nt, preferred_element_type=F32
    )
    early_ref[total:, :] = jnp.zeros((SEG, 2 * wide), F32)
    act_ref[...] = lax.dot_general(
        rows_ref[:own_class, :], weight_ref[2 * wide :, :], nt, preferred_element_type=F32
    )
    is_filter = lax.axis_index("fsdp") < lax.axis_size("fsdp") // 2
    for segment in range(own_class // SEG):
        at = segment * SEG
        source = table_ref[me ^ (2 * (segment // seg_count)), segment % seg_count]
        found = place(jnp.maximum(source, 0), seg_count, peers // 2, me)
        source = pl.multiple_of(jnp.where(source >= 0, found * SEG, total), SEG)
        carried = early_ref[pl.ds(source, SEG), :]
        preact = (
            act_ref[at : at + SEG, :]
            + carried[:, :wide]
            + roll_half(carried[:, wide:], early_ref[at : at + SEG, wide:])
        )
        act_ref[at : at + SEG, :] = jnp.where(is_filter, jnp.tanh(preact), jax.nn.sigmoid(preact))
    sent_ref[:own_class, :] = act_ref[...].astype(BF16)
    sent_ref[own_class:, :] = grad_ref[...]


def gate(act_ref, other_ref, *refs):
    grads, outs, pre_ref = list(refs[:-3]), refs[-3:-1], refs[-1]
    count = outs[0].shape[0]
    is_filter = lax.axis_index("fsdp") < lax.axis_size("fsdp") // 2
    slots = len(grads) + 1
    grads.insert(slots // 2, other_ref.at[slots * count :, :])
    for slot, grad in enumerate(grads):
        at = slot * count
        there = (slot ^ (slots // 2)) * count
        mine = act_ref[at : at + count, :]
        theirs = other_ref[there : there + count, :].astype(F32)
        upstream = grad[...].astype(F32)
        if slot < len(outs):
            outs[slot][...] = (mine * theirs).astype(BF16)
        for_filter = upstream * theirs * (1.0 - mine * mine)
        for_gate = upstream * theirs * mine * (1.0 - mine)
        pre_ref[at : at + count, :] = jnp.where(is_filter, for_filter, for_gate).astype(BF16)


def input_grad(follow_ref, own_ref, other_ref, weight_ref, gated_ref, *refs):
    sends, here_ref, pre_ref, routed_ref = refs[:-3], refs[-3], refs[-2], refs[-1]
    total, wide = own_ref.shape
    width = wide // 2
    pre_ref[:total, :] = own_ref[...].astype(F32)
    pre_ref[total : 2 * total, :width] = other_ref[:, width:].astype(F32)
    pre_ref[total : 2 * total, width:] = other_ref[:, :width].astype(F32)
    pre_ref[2 * total :, :] = jnp.zeros((SEG, wide), F32)
    for segment in range(total // SEG):
        at = segment * SEG
        follow = pl.multiple_of(follow_ref[segment] * SEG, SEG)
        carried = pre_ref[pl.ds(follow, SEG), :]
        local = pre_ref[at : at + SEG, :]
        routed_ref[at : at + SEG, :wide] = carried
        routed_ref[at : at + SEG, wide : 2 * wide] = roll_half(local, carried)
        routed_ref[at : at + SEG, 2 * wide :] = local
    count = here_ref.shape[0]
    fold = C // wide
    for i in range(fold):
        piece = gated_ref[i * (count // fold) : (i + 1) * (count // fold), :]
        sends[0][count:, i * wide : (i + 1) * wide] = piece
    routed = routed_ref[...].astype(BF16)
    here_ref[...] = routed[:count, :]
    part = jnp.dot(routed[count:, :], weight_ref[...], preferred_element_type=F32)
    for slot, out in enumerate(sends):
        out[:count, :] = part[slot * count : (slot + 1) * count, :].astype(BF16)


def spread(own_ref, other_ref, row_ref, copies_ref):
    total, wide = own_ref.shape
    width = wide // 2
    for copy in range(copies_ref.shape[0]):
        copies_ref[copy, :total, :] = own_ref[:, :width]
        copies_ref[copy, total : 2 * total, :] = other_ref[:, width:]
        copies_ref[copy, 2 * total :, :] = row_ref[...]


def local(here_ref, weight_ref, out_ref):
    out_ref[...] = jnp.dot(here_ref[...], weight_ref[...], preferred_element_type=F32)


def mark(out_ref):
    out_ref[...] = jnp.zeros(out_ref.shape, out_ref.dtype)


def nothing(*refs):
    pass


def held(values, after):
    return pl.pallas_call(
        nothing,
        out_shape=[shaped(value.shape, value.dtype) for value in values],
        in_specs=[ANY] * (len(values) + len(after)),
        out_specs=[ANY] * len(values),
        input_output_aliases={i: i for i in range(len(values))},
        compiler_params=pltpu.CompilerParams(vmem_limit_bytes=2**20),
        cost_estimate=pl.CostEstimate(flops=10000000, bytes_accessed=0, transcendentals=0),
    )(*values, *after)


def weight_grad(scale, pre_ref, *refs):
    blocks = refs[:-10]
    out_ref, total_ref, early_ref, routed_ref, rows_ref, wide_ref, follow_ref, sem, sems, out_sems = refs[-10:]
    groups, total, width = early_ref.shape
    total -= SEG
    for i in range(groups):
        wide_ref[i] = pre_ref[lax.axis_index("dp") ^ i, total:, :].astype(F32).astype(jnp.int32)
    load = pltpu.make_async_copy(wide_ref, follow_ref, sem)
    load.start()
    loads = []
    count = blocks[0].shape[0]
    for i in LOADED:
        rows = pl.ds(i * count, count)
        loads.append(pltpu.make_async_copy(blocks[i], rows_ref.at[rows, :], sems.at[i]))
        loads[-1].start()
    for i, block in enumerate(blocks):
        if i not in LOADED:
            rows_ref[i * count : (i + 1) * count, :] = block[...]
    for i in range(groups):
        early_ref[i, :total, :] = pre_ref[lax.axis_index("dp") ^ i, :total, :].astype(F32)
        early_ref[i, total:, :] = jnp.zeros((SEG, width), F32)
    load.wait()
    for i in range(groups):
        for segment in range(total // SEG):
            at = segment * SEG
            follow = pl.multiple_of(follow_ref[i, 0, segment] * SEG, SEG)
            carried = early_ref[i, pl.ds(follow, SEG), :]
            local = early_ref[i, at : at + SEG, :]
            at += i * total
            routed_ref[at : at + SEG, :width] = carried
            routed_ref[at : at + SEG, width : 2 * width] = roll_half(local, carried)
            routed_ref[at : at + SEG, 2 * width :] = local
    routed = routed_ref[...].astype(BF16)
    for one in loads:
        one.wait()
    half = C // 2
    stores = []
    for part in range(2):
        product = lax.dot_general(
            routed,
            rows_ref[:, part * half : (part + 1) * half],
            (((0,), (0,)), ((), ())),
            preferred_element_type=F32,
        )
        for tap in range(3):
            start = tap * C + part * half
            here = pl.ds(start, half)
            total_ref[:, start : start + half] = product[tap * width : (tap + 1) * width, :] * scale
            stores.append(pltpu.make_async_copy(total_ref.at[:, here], out_ref.at[:, here], out_sems.at[len(stores)]))
            stores[-1].start()
    for one in stores:
        one.wait()


def finish(kept_ref, gated_ref, *refs):
    parts, (grad_ref, out_ref) = refs[:-2], refs[-2:]
    count = grad_ref.shape[0]
    total = kept_ref[...]
    for part in parts:
        total = total + part[:count, :].astype(F32)
    grad_ref[...] = total.astype(BF16)
    wide = gated_ref.shape[1]
    width = wide // 2
    fold = C // wide
    short = count // fold
    q = lax.rem(lax.axis_index("fsdp"), out_ref.shape[1] // width)
    for part in range(2):
        here = slice(part * width, (part + 1) * width)
        out_ref[:, pl.ds(pl.multiple_of((q ^ part) * width, width), width)] = gated_ref[:, here]
        start = pl.multiple_of((q ^ (2 + part)) * width, width)
        for i in range(fold):
            piece = parts[0][count:, i * wide + part * width : i * wide + (part + 1) * width]
            out_ref[i * short : (i + 1) * short, pl.ds(start, width)] = piece


def by_channels(signal, grad_gated, conv_weight, source_seg):
    peers, groups = lax.axis_size("fsdp"), lax.axis_size("dp")
    chips = peers // 2
    seg_count = source_seg.shape[1]
    rows, width = signal.shape[0], conv_weight.shape[0]
    own_class, all_rows = chips * rows, peers * rows
    wide = 2 * width
    half_chips = chips // 2

    fold = C // wide
    own_rows = [signal] + [swap(signal, "fsdp", 2 * k) for k in range(1, chips)]
    picked = call(
        pick, [shaped((rows, wide), BF16)] * half_chips, [grad_gated], [VMEM]
    )
    other_weight = swap(conv_weight, "fsdp", 1)
    weight = call(
        stack_weight, [shaped((3 * wide, C), BF16)], [conv_weight, other_weight], [VMEM] * 2
    )[0]
    table = exchange(jnp.broadcast_to(source_seg[None], (peers, 1, seg_count)), "fsdp").reshape(peers, seg_count)
    grads = [picked[0], swap(picked[1], "fsdp", 2), swap(picked[1], "fsdp", 6)]
    own_stack = call(
        stack, [shaped((own_class, C), BF16)], own_rows, [VMEM] * chips, after=[table, picked[0]]
    )[0]
    other_stack = swap(own_stack, "fsdp", 1)
    act, sent = call(
        forward,
        [shaped((own_class, wide), F32), shaped((own_class + rows, wide), BF16)],
        [table, weight, own_stack, other_stack, picked[0]],
        [SMEM] + [VMEM] * 4,
        [pltpu.VMEM((all_rows, C), BF16), pltpu.VMEM((all_rows + SEG, 2 * wide), F32)],
        after=grads[1:],
    )
    partner = swap(sent, "fsdp", peers // 2)
    far_own = [swap(own_stack, "dp", d) for d in (1, 2, 3)]
    follow, follow_row = call(
        functools.partial(follows, chips),
        [shaped((peers * seg_count + 1,), jnp.int32), shaped((16, width), BF16)],
        [table],
        [SMEM],
        out_specs=[SMEM, VMEM],
        after=[sent],
    )

    *gated, pre = call(
        gate,
        [shaped((rows, wide), BF16)] * half_chips + [shaped((own_class, wide), BF16)],
        [act, partner, *grads],
        [VMEM] * (2 + len(grads)),
    )
    other_pre = swap(pre, "fsdp", 1)
    *sends, here = call(
        input_grad,
        [shaped((rows + rows // fold, C), BF16)]
        + [shaped((rows, C), BF16)] * (chips - 2)
        + [shaped((rows, 3 * wide), BF16)],
        [follow, pre, other_pre, weight, gated[1]],
        [SMEM, VMEM, VMEM, VMEM, VMEM],
        [pltpu.VMEM((all_rows + SEG, wide), F32), pltpu.VMEM((own_class, 3 * wide), F32)],
    )
    parts = [swap(part, "fsdp", 2 * (k + 1)) for k, part in enumerate(sends)]
    sent_pre = call(
        spread,
        [shaped((groups, all_rows + 16, width), BF16)],
        [pre, other_pre, follow_row],
        [VMEM] * 3,
    )[0]
    all_pre = exchange(sent_pre, "dp")
    kept = call(
        local, [shaped((rows, C), F32)], [here, weight], [VMEM] * 2, after=[sent_pre]
    )[0]
    arrived = call(mark, [shaped((8, 128), F32)], [], [], after=[kept, *far_own])[0]
    grad_in, gated_out = call(
        finish,
        [shaped((rows, C), BF16), shaped((rows, H), BF16)],
        [kept, gated[0], *parts],
        [VMEM] * (chips + 1),
        after=[arrived],
    )
    far_own = held(far_own, [arrived])
    far_other = [swap(block, "fsdp", 1) for block in far_own]
    blocks = [own_stack, other_stack] + [block for pair in zip(far_own, far_other) for block in pair]
    grad_weight = call(
        functools.partial(weight_grad, 1.0 / math.sqrt(all_rows * groups)),
        [shaped((width, 3 * C), F32)],
        [all_pre, *blocks],
        [VMEM] + [ANY if i in LOADED else VMEM for i in range(len(blocks))],
        [
            pltpu.VMEM((width, 3 * C), F32),
            pltpu.VMEM((groups, all_rows + SEG, width), F32),
            pltpu.VMEM((groups * all_rows, 3 * width), F32),
            pltpu.VMEM((groups * all_rows, C), BF16),
            pltpu.VMEM((groups, 16, width), jnp.int32),
            pltpu.SMEM((groups, 16, width), jnp.int32),
            pltpu.SemaphoreType.DMA,
            pltpu.SemaphoreType.DMA((len(blocks),)),
            pltpu.SemaphoreType.DMA((6,)),
        ],
        out_specs=[ANY],
        room=24,
    )[0]
    return gated_out, grad_in, grad_weight


def tap_starts(context_row_block):
    return [context_row_block - (2 - selected_index) * DILATION_SIZE for selected_index in range(3)]


def by_rows(signal, grad_gated, conv_weight, source_seg):
    peer_count = lax.axis_size("fsdp")
    seg_count = source_seg.shape[1]
    row_count = signal.shape[0]
    seg_rows = row_count // seg_count
    context_row_block = 2 * DILATION_SIZE
    starts = tap_starts(context_row_block)
    segments = signal.reshape(seg_count, seg_rows, C)
    sources = source_seg[0]
    source_dev = jnp.where(sources >= 0, sources // seg_count, -1)
    peers = jnp.arange(peer_count, dtype=jnp.int32)
    request_mask = (source_dev[None, :] == peers[:, None]).astype(jnp.int32)
    asked = lax.all_to_all(request_mask, "fsdp", split_axis=0, concat_axis=0, tiled=True)
    send_table = asked.astype(jnp.bfloat16)
    recv_table = (source_dev[:, None] == peers[None, :]).astype(jnp.bfloat16)
    outgoing = jnp.einsum(
        "ns,slc->nlc", send_table, segments, preferred_element_type=jnp.float32
    ).astype(jnp.bfloat16)
    incoming = lax.all_to_all(outgoing, "fsdp", split_axis=0, concat_axis=0, tiled=True)
    carries = jnp.einsum(
        "sn,nlc->slc", recv_table, incoming, preferred_element_type=jnp.float32
    ).astype(jnp.bfloat16)
    extended = jnp.concatenate([carries, segments], axis=1)
    full_weight = lax.all_gather(conv_weight, "fsdp", axis=0, tiled=True)
    contract_final_axis = (((1,), (1,)), ((), ()))
    contract_first = (((0,), (0,)), ((), ()))
    windows = [extended[:, start : start + seg_rows, :].reshape(row_count, C) for start in starts]
    preact = sum(
        (
            lax.dot_general(
                windows[selected_index],
                full_weight[:, selected_index * C : (selected_index + 1) * C],
                contract_final_axis,
                preferred_element_type=jnp.float32,
            )
            for selected_index in range(3)
        )
    )
    filter_act = jnp.tanh(preact[:, :H])
    gate_act = jax.nn.sigmoid(preact[:, H:])
    gated_out = (filter_act * gate_act).astype(jnp.bfloat16)
    upstream_wide = grad_gated.astype(jnp.float32)
    grad_pre = jnp.concatenate(
        [
            upstream_wide * gate_act * (1.0 - filter_act * filter_act),
            upstream_wide * filter_act * gate_act * (1.0 - gate_act),
        ],
        axis=1,
    ).astype(jnp.bfloat16)
    partial_value = jnp.concatenate(
        [
            lax.dot_general(
                grad_pre,
                windows[selected_index],
                contract_first,
                preferred_element_type=jnp.float32,
            ).astype(jnp.bfloat16)
            for selected_index in range(3)
        ],
        axis=1,
    )
    arrived = lax.all_to_all(partial_value, "fsdp", split_axis=0, concat_axis=0, tiled=True)
    shard_sum = jnp.sum(arrived.reshape(peer_count, -1, 3 * C), axis=0, dtype=jnp.float32)
    group_total = lax.psum(shard_sum, "dp")
    total_token_count = row_count * peer_count * lax.axis_size("dp")
    grad_weight = group_total * (1.0 / math.sqrt(total_token_count))
    back_proj = jnp.dot(grad_pre, full_weight, preferred_element_type=jnp.float32)
    back_proj = back_proj.reshape(seg_count, seg_rows, 3 * C)
    grad_ext = jnp.zeros((seg_count, context_row_block + seg_rows, C), jnp.float32)
    for selected_index, start in enumerate(starts):
        grad_ext = grad_ext.at[:, start : start + seg_rows, :].add(
            back_proj[:, :, selected_index * C : (selected_index + 1) * C]
        )
    outgoing_grad = jnp.einsum(
        "sn,slc->nlc",
        recv_table.astype(jnp.float32),
        grad_ext[:, :context_row_block, :],
        precision=lax.Precision.HIGHEST,
    )
    incoming_grad = lax.all_to_all(outgoing_grad, "fsdp", split_axis=0, concat_axis=0, tiled=True)
    tail_grad = jnp.einsum(
        "ns,nlc->slc",
        send_table.astype(jnp.float32),
        incoming_grad,
        precision=lax.Precision.HIGHEST,
    )
    grad_in = (
        grad_ext[:, context_row_block:, :].at[:, seg_rows - context_row_block :, :].add(tail_grad)
    )
    grad_in = grad_in.reshape(row_count, C).astype(jnp.bfloat16)
    return (gated_out, grad_in, grad_weight)


def per_device(signal, grad_gated, conv_weight, source_seg):
    peers, groups = lax.axis_size("fsdp"), lax.axis_size("dp")
    rows, seg_count = signal.shape[0], source_seg.shape[1]
    fits = (
        rows == SEG * seg_count
        and conv_weight.shape[0] % 128 == 0
        and peers & (peers - 1) == 0
        and groups & (groups - 1) == 0
        and peers == 8
        and groups == 4
        and groups * peers * rows <= 2048
        and rows % 64 == 0
        and peers * seg_count <= 128
        and seg_count & (seg_count - 1) == 0
    )
    plan = by_channels if fits else by_rows
    return plan(signal, grad_gated, conv_weight, source_seg)


def solution(mesh):
    placed = (
        P(("dp", "fsdp"), None),
        P(("dp", "fsdp"), None),
        P("fsdp", None),
        P(("dp", "fsdp"), None),
    )
    return jax.shard_map(
        per_device,
        mesh=mesh,
        in_specs=placed,
        out_specs=(P(("dp", "fsdp"), None), P(("dp", "fsdp"), None), P("fsdp", None)),
        check_vma=False,
    )
```
